256 devices in a mesh: expert: 16 (over z, x_lo), tensor: 16 (over x_hi, y, core).
Axes of the slice: x: 4 (x_hi: 2, x_lo: 2; x = x_hi * 2 + x_lo), y: 4, z: 8, core: 2. Of those that a mesh axis runs over, the one named last changes fastest.
Arguments:
- context: bfloat16 [2048, 8192], P('expert', 'tensor'), may hold values from -6 to 6
- proj_weight: bfloat16 [8192, 4096], P('tensor', 'expert'), may hold values from -0.0625 to 0.0625
- norm_gain: float32 [4096], replicated, may hold values from 0.1 to 1.9
- expert_ids: int32 [2048, 8], P(('expert', 'tensor')), may hold values from 0 to 63, all different within a row; in each aligned block of 8 rows (0 to 7, 8 to 15, ...) at most 2 rows name the same one
- gate_values: float32 [2048, 8], P(('expert', 'tensor')), may hold values from 0.1 to 1
- w_gate: bfloat16 [256, 4096, 384], P(('expert', 'tensor')), may hold values from -0.09375 to 0.09375
- w_up: bfloat16 [256, 4096, 384], P(('expert', 'tensor')), may hold values from -0.09375 to 0.09375
- w_down: bfloat16 [256, 384, 4096], P(('expert', 'tensor')), may hold values from -0.15625 to 0.15625
Outputs:
- mixed: bfloat16 [2048, 4096], P(('expert', 'tensor'))
The draws below stay inside these ranges and needn't reach their ends.
Inputs may be any that keep to these rules, and one draw needn't show every extreme that they name: `expert_ids`: each row names 8 different experts. The tokens fall into aligned blocks of 8 rows, block b holding tokens b * 8 to (b + 1) * 8 - 1; in every block no expert is named by more than 2 rows, a bound that some block reaches.
All inputs are finite; a program needn't handle non-finite values.
Results may differ from the reference program's by a relative error of at most 0.024.
Values may be sent and summed in bfloat16 or wider, within the bound.
No kernel may reach another device: no remote copies, remote signals or barrier semaphores. Data moves between devices by JAX's collectives and lax.ppermute only.
A program may use at most 128 MiB of HBM per device.

```python
import math
import jax
import jax.numpy as jnp
import numpy as np
from jax import lax

D = 4096
HQ = 64
HD = 128
FF = 1536
TOPK = 8
TOK_DEV = 128
TOKENS = 2048
ROW_DEV = 8
EXPERTS = 64
CAP = 2
N_TENSOR = 16


def level_of(own_key, shape, shards, least, high):
    def one(axis_at, parts):
        heights = jax.random.uniform(jax.random.fold_in(jax.random.fold_in(own_key, 6), axis_at), (parts,), jnp.float32, least / len(shards), high / len(shards))
        return jnp.repeat(jnp.exp(heights), shape[axis_at] // parts).reshape((-1,) + (1,) * (len(shape) - axis_at - 1))

    level = one(*shards[0])
    for cut in shards[1:]:
        level = level * one(*cut)
    return level


def routed_block(own_key, own, number, rows, amount, top, limit, lean):
    order = jax.random.permutation(own_key, amount)
    heavy_load, common = shares(amount, rows * top, limit, lean, True), shares(amount, rows * top, limit, lean, False)
    places = jnp.arange(amount)

    def named(tallies, turn):
        used = int((tallies > 0).sum())
        fixed = max(1, used // 4)
        passed = fixed + (places - fixed + turn * (used - fixed)) % max(1, amount - fixed)
        return jnp.zeros((amount,), jnp.int32).at[order[jnp.where(places < fixed, places, passed)]].set(jnp.asarray(tallies, jnp.int32))

    tallies = jnp.where(number % 4 == 0, named(heavy_load, number // 4), named(common, number - number // 4 - 1))
    mixed = jax.random.permutation(jax.random.fold_in(own, 3), amount)
    donor, sink = mixed[0:amount // 2 * 2:2], mixed[1:amount // 2 * 2:2]
    room = jnp.minimum(tallies[donor] - 1, limit - tallies[sink]) // 2
    room = jnp.where((donor == order[0]) | (sink == order[0]) | (tallies[sink] == 0), 0, jnp.maximum(room, 0))
    passed = jax.random.randint(jax.random.fold_in(own, 4), (amount // 2,), 0, 1 << 20) % (room + 1)
    tallies = tallies.at[donor].add(-passed).at[sink].add(passed)
    items = jnp.searchsorted(jnp.cumsum(tallies), jnp.arange(rows * top), side="right").astype(jnp.int32)
    listing = items.reshape(top, rows).T
    listing = listing[jax.random.permutation(jax.random.fold_in(own, 1), rows)]
    turn = jax.random.randint(jax.random.fold_in(own, 2), (rows, 1), 0, top)
    return jnp.take_along_axis(listing, (jnp.arange(top)[None, :] + turn) % top, axis=1)


def shares(amount, total, reach, slope, full):
    weights = [(1 << 20) // math.isqrt(rank ** slope) + 1 for rank in range(1, amount + 1)]
    largest = reach if full else min(reach, max(-(-total // amount), total * weights[0] // sum(weights)))
    least = 1 if total - largest >= amount - 1 else 0
    given, spare = [largest] + [least] * (amount - 1), total - largest - least * (amount - 1)
    while spare > 0:
        free = [i for i in range(1, amount) if given[i] < largest] or [i for i in range(1, amount) if given[i] < reach]
        pool, remaining = sum([weights[i] for i in free]), spare
        for i in free:
            addition = min(reach - given[i], max(1, remaining * weights[i] // pool), spare)
            given[i] = given[i] + addition
            spare = spare - addition
    return np.array(given)


def gaussian(stream_key, dims, spread, limit, shards=(), kind=jnp.bfloat16):
    drawn = jax.random.normal(stream_key, dims, jnp.float32) * spread
    if len(shards) > 0:
        drawn = level_of(stream_key, dims, shards, -0.22, 0.18) * drawn
    return jnp.clip(drawn, min=-limit, max=limit).astype(kind)


def setup_inputs(seed: int = 0) -> dict:
    arg_keys = jax.random.split(jax.random.key(seed), 9)
    context = gaussian(arg_keys[0], (TOKENS, HQ * HD), 1.0, 6.0, ((0, 16), (1, 16)))
    proj_weight = gaussian(arg_keys[1], (HQ * HD, D), (HQ * HD) ** -0.5, 0.0625, ((0, 16), (1, 16)))
    norm_gain = jnp.clip(1.0 + 0.18 * jax.random.normal(arg_keys[2], (D,), jnp.float32), 0.1, 1.9)
    expert_ids_keys = jax.random.split(jax.random.fold_in(arg_keys[3], 1), TOKENS // ROW_DEV)
    expert_ids_turns = jax.random.permutation(jax.random.fold_in(arg_keys[3], 3), TOKENS // ROW_DEV)
    expert_ids = jax.vmap(lambda own, number: routed_block(jax.random.fold_in(arg_keys[3], 2), own, number, ROW_DEV, EXPERTS, TOPK, CAP, 2))(expert_ids_keys, expert_ids_turns).reshape((TOKENS, TOPK))
    gate_values = jnp.clip(0.1 + 0.9 * jax.random.uniform(arg_keys[4], (TOKENS, TOPK), jnp.float32) ** level_of(arg_keys[4], (TOKENS, TOPK), ((0, 256),), -0.2, 0.2), 0.1, 1.0)
    w_gate = gaussian(arg_keys[5], (EXPERTS * 4, D, FF // 4), D ** -0.5, 0.09375, ((0, 256),))
    w_up = gaussian(arg_keys[6], (EXPERTS * 4, D, FF // 4), D ** -0.5, 0.09375, ((0, 256),))
    w_down = gaussian(arg_keys[7], (EXPERTS * 4, FF // 4, D), FF ** -0.5, 0.15625, ((0, 256),))
    return {"context": context, "proj_weight": proj_weight, "norm_gain": norm_gain, "expert_ids": expert_ids, "gate_values": gate_values, "w_gate": w_gate, "w_up": w_up, "w_down": w_down}


def expert_rows(inputs, gate_part, up_part, down_part):
    running = jnp.zeros((inputs.shape[0], down_part.shape[2]), jnp.float32)
    for quarter in range(4):
        gate_act = jnp.dot(inputs, gate_part[quarter], preferred_element_type=jnp.float32)
        up_act = jnp.dot(inputs, up_part[quarter], preferred_element_type=jnp.float32)
        hidden = (jax.nn.silu(gate_act) * up_act).astype(jnp.bfloat16)
        partial_out = jnp.dot(hidden, down_part[quarter], preferred_element_type=jnp.float32).astype(jnp.bfloat16)
        running = running + partial_out.astype(jnp.float32)
    return running.astype(jnp.bfloat16)

def reference(context, proj_weight, norm_gain, expert_ids, gate_values, w_gate, w_up, w_down):
    attended = jnp.dot(context, proj_weight, preferred_element_type=jnp.float32).astype(jnp.bfloat16)
    stream = attended.astype(jnp.float32)
    scale = lax.rsqrt(lax.optimization_barrier(jnp.mean(stream * stream, axis=-1, keepdims=True)) + 1e-06)
    normed = (stream * scale * norm_gain).astype(jnp.bfloat16)
    token_count = stream.shape[0]
    block_rows = TOK_DEV // N_TENSOR
    block_count = token_count // block_rows
    labels = jnp.arange(EXPERTS, dtype=jnp.int32)
    matches = expert_ids[:, :, None] == labels[None, None, :]
    choose = lax.optimization_barrier(jnp.sum(matches.astype(jnp.int32), axis=1))
    weights = lax.optimization_barrier(jnp.sum(jnp.where(matches, gate_values[:, :, None], 0.0), axis=1))
    per_block = choose.reshape(block_count, block_rows, EXPERTS)
    slot_rank = jnp.cumsum(per_block, axis=1) - per_block
    base = (jnp.arange(block_count, dtype=jnp.int32) * CAP)[:, None, None]
    position = (base + slot_rank).reshape(token_count, EXPERTS).astype(jnp.int32)
    gate_all = w_gate.reshape(EXPERTS, 4, w_gate.shape[1], w_gate.shape[2])
    up_all = w_up.reshape(EXPERTS, 4, w_up.shape[1], w_up.shape[2])
    down_all = w_down.reshape(EXPERTS, 4, w_down.shape[1], w_down.shape[2])
    slots_all = block_count * CAP

    def expert_step(running, members):
        gate_part, up_part, down_part, chosen, where_at, weight_col = members
        dest_index = jnp.where(chosen > 0, where_at, slots_all).astype(jnp.int32)
        buffer = jnp.zeros((slots_all, normed.shape[1]), jnp.bfloat16).at[dest_index].set(normed, mode='drop')
        outputs = expert_rows(buffer, gate_part, up_part, down_part)
        fetched = jnp.take(outputs, jnp.minimum(dest_index, slots_all - 1), axis=0).astype(jnp.float32)
        return (running + weight_col[:, None] * fetched, None)
    members = (gate_all, up_all, down_all, choose.T, position.T, weights.T)
    mixture, _ = lax.scan(expert_step, jnp.zeros(stream.shape, jnp.float32), members)
    return (stream + mixture).astype(jnp.bfloat16)
```

```python
import jax
import jax.numpy as jnp
from jax import lax
from jax.sharding import Mesh
from jax.sharding import PartitionSpec as P

TOPK = 8
QUARTERS = 4
CAP = 2

FINE = ("z", "xl", "xh", "y", "c")
SIZES = (8, 2, 2, 4, 2)
EXPERT = ("z", "xl")
TENSOR = ("xh", "y", "c")
PLANE = ("xh", "y")
NZ = 8


def swap(x, axis):
    return lax.ppermute(x, axis, [(0, 1), (1, 0)])


def fetch(x, hop):
    return lax.ppermute(x, "z", [((i + hop) % NZ, i) for i in range(NZ)])


def gather_z(x):
    up1, dn1 = fetch(x, 1), fetch(x, -1)
    up2, dn2 = fetch(x, 2), fetch(x, -2)
    up3, dn3 = fetch(up1, 2), fetch(dn1, -2)
    far = fetch(up3, 1)
    return [x, up1, up2, up3, far, dn3, dn2, dn1]


def expert_rows(rows, w_gate, w_up, w_down):
    gate_act = jnp.dot(rows, w_gate, preferred_element_type=jnp.float32)
    up_act = jnp.dot(rows, w_up, preferred_element_type=jnp.float32)
    hidden = (jax.nn.silu(gate_act) * up_act).astype(jnp.bfloat16)
    return jnp.dot(hidden, w_down, preferred_element_type=jnp.float32)


def on_device(context, proj_weight, norm_gain, expert_ids, gate_values, w_gate, w_up, w_down):
    zi, xli = lax.axis_index("z"), lax.axis_index("xl")
    n_tensor = lax.axis_size(TENSOR)
    n_plane = lax.axis_size(PLANE)
    n_expert = lax.axis_size(EXPERT)
    rows = context.shape[0] // n_tensor
    groups = n_tensor // QUARTERS
    cols = proj_weight.shape[1]
    width = cols * n_expert
    tokens = rows * n_expert

    routing = jnp.concatenate([expert_ids.astype(jnp.float32), gate_values], axis=1)
    routing = lax.all_gather(routing, EXPERT, axis=0, tiled=True)

    other = swap(proj_weight, "xl")
    blocks = [b.reshape(n_tensor, 1, rows, -1) for b in gather_z(context)]
    lhs = jnp.concatenate(blocks, axis=1).reshape(NZ * context.shape[0], -1)
    rhs = jnp.concatenate([proj_weight, other], axis=1)
    partial = jnp.dot(lhs, rhs, preferred_element_type=jnp.float32).astype(jnp.bfloat16)
    partial = partial.reshape(n_tensor, NZ * rows, 2 * cols)
    partial = lax.all_to_all(partial, TENSOR, 0, 0, tiled=True)
    part = jnp.sum(partial.astype(jnp.float32), axis=0).astype(jnp.bfloat16)
    part = jnp.where(xli == 0, part, jnp.concatenate([part[:, cols:], part[:, :cols]], axis=1))

    mate = swap(part, "xl")
    part = part.reshape(NZ, 1, rows, 2 * cols)
    mate = mate.reshape(NZ, 1, rows, 2 * cols)
    pair = jnp.where(
        xli == 0, jnp.concatenate([part, mate], axis=1), jnp.concatenate([mate, part], axis=1)
    )
    start = lax.rem(NZ - zi, NZ)
    pair = lax.dynamic_slice_in_dim(jnp.concatenate([pair, pair], axis=0), start, NZ, axis=0)
    pair = pair.reshape(tokens, 2 * cols)
    attended = jnp.zeros((tokens, width), jnp.bfloat16)
    for hop, block in enumerate(gather_z(pair)):
        at = lax.rem(zi + hop, NZ) * (2 * cols)
        attended = lax.dynamic_update_slice_in_dim(attended, block, at, axis=1)
    stream = attended.astype(jnp.float32)
    scale = lax.rsqrt(jnp.mean(stream * stream, axis=-1, keepdims=True) + 1e-06)
    normed = (stream * scale * norm_gain).astype(jnp.bfloat16)

    ids = routing[:, :TOPK].astype(jnp.int32)
    gates = routing[:, TOPK:]
    ei = zi * 2 + xli
    labels = ei * groups + jnp.arange(groups, dtype=jnp.int32)
    match = ids[:, :, None] == labels[None, None, :]
    chosen = jnp.sum(match.astype(jnp.int32), axis=1)
    weight = jnp.sum(jnp.where(match, gates[:, :, None], 0.0), axis=1)
    blocked = chosen.reshape(n_expert, rows, groups)
    rank = (jnp.cumsum(blocked, axis=1) - blocked).reshape(tokens, groups)
    base = (jnp.arange(tokens, dtype=jnp.int32) // rows) * CAP
    slot = jnp.where(chosen > 0, base[:, None] + rank, -1)
    slots = n_expert * CAP
    placing = slot[:, :, None] == jnp.arange(slots, dtype=jnp.int32)[None, None, :]
    placing = jnp.repeat(placing, n_plane // groups, axis=1).reshape(tokens, n_plane * slots)
    weight = jnp.repeat(weight, n_plane // groups, axis=1)
    weight = jnp.where(placing, jnp.repeat(weight, slots, axis=1), 0.0)

    sent = lax.dot_general(
        placing.astype(jnp.bfloat16),
        normed,
        (((0,), (0,)), ((), ())),
        preferred_element_type=jnp.float32,
    ).astype(jnp.bfloat16)
    sent = sent.reshape(n_plane, slots, width)
    mine = lax.all_to_all(sent, PLANE, 0, 0, tiled=True).reshape(n_plane * slots, width)
    theirs = swap(mine, "c")
    theirs_out = expert_rows(theirs, w_gate[0], w_up[0], w_down[0]).astype(jnp.bfloat16)
    from_mate = swap(theirs_out, "c")
    mine_out = expert_rows(mine, w_gate[0], w_up[0], w_down[0])
    summed = (mine_out + from_mate.astype(jnp.float32)).astype(jnp.bfloat16)
    summed = summed.reshape(n_plane, slots, width)
    back = lax.all_to_all(summed, PLANE, 0, 0, tiled=True).reshape(n_plane * slots, width)

    high = weight.astype(jnp.bfloat16)
    low = (weight - high.astype(jnp.float32)).astype(jnp.bfloat16)
    mixture = jnp.dot(high, back, preferred_element_type=jnp.float32) + jnp.dot(
        low, back, preferred_element_type=jnp.float32
    )
    mixture = mixture.astype(jnp.bfloat16).reshape(NZ, 2, rows, width)
    keep = lax.dynamic_index_in_dim(mixture, xli, 1, keepdims=False)
    give = lax.dynamic_index_in_dim(mixture, 1 - xli, 1, keepdims=False)
    got = swap(give, "xl")
    half = (keep.astype(jnp.float32) + got.astype(jnp.float32)).astype(jnp.bfloat16)
    home = lax.all_to_all(half, "z", 0, 0, tiled=True)
    own = lax.dynamic_slice_in_dim(attended, ei * rows, rows, axis=0)
    out = own.astype(jnp.float32) + jnp.sum(home.astype(jnp.float32), axis=0)
    return out.astype(jnp.bfloat16)


def solution(mesh):
    fine = Mesh(mesh.devices.reshape(SIZES), FINE)
    both = EXPERT + TENSOR
    return jax.shard_map(
        on_device,
        mesh=fine,
        in_specs=(
            P(EXPERT, TENSOR),
            P(TENSOR, EXPERT),
            P(),
            P(both, None),
            P(both, None),
            P(both, None, None),
            P(both, None, None),
            P(both, None, None),
        ),
        out_specs=P(both, None),
        check_vma=False,
    )
```

```python
import jax
import jax.numpy as jnp
from jax import lax
from jax.sharding import Mesh
from jax.sharding import PartitionSpec as P

TOPK = 8
CAP = 2

FINE = ("z", "xl", "xh", "y", "c")
SIZES = (8, 2, 2, 4, 2)
EXPERT = ("z", "xl")
TENSOR = ("xh", "y", "c")
SPREAD = ("xh", "y")
PLANE = ("xl", "xh", "y")
NZ = 8


def swap(x, axis):
    return lax.ppermute(x, axis, [(0, 1), (1, 0)])


def fetch(x, hop):
    return lax.ppermute(x, "z", [((i + hop) % NZ, i) for i in range(NZ)])


def gather_z(x):
    up1, dn1 = fetch(x, 1), fetch(x, -1)
    up2, dn2 = fetch(x, 2), fetch(x, -2)
    up3, dn3 = fetch(up1, 2), fetch(dn1, -2)
    far = fetch(up3, 1)
    return [x, up1, up2, up3, far, dn3, dn2, dn1]


def settle_z(blocks, zi):
    twice = jnp.stack(blocks + blocks, axis=0)
    return lax.dynamic_slice_in_dim(twice, lax.rem(NZ - zi, NZ), NZ, axis=0)


def hidden_rows(rows, w_gate, w_up):
    gate_act = jnp.dot(rows, w_gate, preferred_element_type=jnp.float32)
    up_act = jnp.dot(rows, w_up, preferred_element_type=jnp.float32)
    return (jax.nn.silu(gate_act) * up_act).astype(jnp.bfloat16)


def on_device(context, proj_weight, norm_gain, expert_ids, gate_values, w_gate, w_up, w_down):
    zi, ci = lax.axis_index("z"), lax.axis_index("c")
    xli = lax.axis_index("xl")
    n_tensor = lax.axis_size(TENSOR)
    n_spread = lax.axis_size(SPREAD)
    n_plane = lax.axis_size(PLANE)
    rows = context.shape[0] // n_tensor
    labels_z = n_plane // 2
    cols = proj_weight.shape[1]
    wide = 2 * cols
    width = NZ * wide
    tokens = NZ * rows

    high = gate_values.astype(jnp.bfloat16)
    low = (gate_values - high.astype(jnp.float32)).astype(jnp.bfloat16)
    note = jnp.concatenate([expert_ids.astype(jnp.bfloat16), high, low], axis=1)
    note = jnp.pad(note, ((0, 0), (0, context.shape[1] - note.shape[1])))
    gathered = gather_z(jnp.concatenate([context, note], axis=0))

    rhs = jnp.concatenate([proj_weight, swap(proj_weight, "xl")], axis=1)
    blocks = [g[: context.shape[0]].reshape(n_spread, 2, 1, rows, -1) for g in gathered]
    lhs = jnp.concatenate(blocks, axis=2)

    def partial_sum(core):
        part = lax.dynamic_index_in_dim(lhs, core, 1, keepdims=False)
        part = part.reshape(n_spread * tokens, -1)
        return jnp.dot(part, rhs, preferred_element_type=jnp.float32)

    got = swap(partial_sum(1 - ci).astype(jnp.bfloat16), "c")
    partial = (partial_sum(ci) + got.astype(jnp.float32)).astype(jnp.bfloat16)
    partial = lax.all_to_all(
        partial.reshape(n_spread, tokens, wide), SPREAD, 0, 0, tiled=True
    )
    part = jnp.sum(partial.astype(jnp.float32), axis=0).astype(jnp.bfloat16)
    part = jnp.where(xli == 0, part, jnp.concatenate([part[:, cols:], part[:, :cols]], axis=1))

    part = settle_z([part[k * rows : (k + 1) * rows] for k in range(NZ)], zi)
    attended = jnp.zeros((tokens, width), jnp.bfloat16)
    for hop, block in enumerate(gather_z(part.reshape(tokens, wide))):
        at = lax.rem(zi + hop, NZ) * wide
        attended = lax.dynamic_update_slice_in_dim(attended, block, at, axis=1)
    stream = attended.astype(jnp.float32)
    scale = lax.rsqrt(jnp.mean(stream * stream, axis=-1, keepdims=True) + 1e-06)
    normed = (stream * scale * norm_gain).astype(jnp.bfloat16)

    notes = settle_z([g[context.shape[0] :, : 3 * TOPK] for g in gathered], zi)
    notes = notes.reshape(tokens, 3 * TOPK).astype(jnp.float32)
    ids = notes[:, :TOPK].astype(jnp.int32)
    gates = notes[:, TOPK : 2 * TOPK] + notes[:, 2 * TOPK :]
    labels = zi * labels_z + jnp.arange(labels_z, dtype=jnp.int32)
    match = ids[:, :, None] == labels[None, None, :]
    chosen = jnp.sum(match.astype(jnp.int32), axis=1)
    weight = jnp.sum(jnp.where(match, gates[:, :, None], 0.0), axis=1)
    blocked = chosen.reshape(NZ, rows, labels_z)
    rank = (jnp.cumsum(blocked, axis=1) - blocked).reshape(tokens, labels_z)
    base = (jnp.arange(tokens, dtype=jnp.int32) // rows) * CAP
    slot = jnp.where(chosen > 0, base[:, None] + rank, -1)
    slots = NZ * CAP
    placing = slot[:, :, None] == jnp.arange(slots, dtype=jnp.int32)[None, None, :]
    placing = jnp.repeat(placing, 2, axis=1).reshape(tokens, n_plane * slots)
    weight = jnp.where(placing, jnp.repeat(weight, 2 * slots, axis=1), 0.0)

    sent = lax.dot_general(
        placing.astype(jnp.bfloat16),
        normed,
        (((0,), (0,)), ((), ())),
        preferred_element_type=jnp.float32,
    ).astype(jnp.bfloat16)
    sent = sent.reshape(n_plane, slots, width)
    mine = lax.all_to_all(sent, PLANE, 0, 0, tiled=True).reshape(n_plane * slots, width)
    theirs = swap(mine, "c")
    mine_hidden = hidden_rows(mine, w_gate[0], w_up[0])
    theirs_hidden = hidden_rows(theirs, w_gate[0], w_up[0])
    theirs_out = jnp.dot(theirs_hidden, w_down[0], preferred_element_type=jnp.float32)
    from_mate = swap(theirs_out.astype(jnp.bfloat16), "c")
    mine_out = jnp.dot(mine_hidden, w_down[0], preferred_element_type=jnp.float32)
    summed = (mine_out + from_mate.astype(jnp.float32)).astype(jnp.bfloat16)
    summed = summed.reshape(n_plane, slots, width)
    back = lax.all_to_all(summed, PLANE, 0, 0, tiled=True).reshape(n_plane * slots, width)

    high = weight.astype(jnp.bfloat16)
    low = (weight - high.astype(jnp.float32)).astype(jnp.bfloat16)
    mixture = jnp.dot(high, back, preferred_element_type=jnp.float32) + jnp.dot(
        low, back, preferred_element_type=jnp.float32
    )
    mixture = mixture.astype(jnp.bfloat16).reshape(NZ, rows, width)
    total = lax.dynamic_slice_in_dim(attended, zi * rows, rows, axis=0).astype(jnp.float32)
    total += lax.dynamic_index_in_dim(mixture, zi, 0, keepdims=False).astype(jnp.float32)
    for hop in (4, 1, 7, 2, 6, 3, 5):
        block = lax.dynamic_index_in_dim(mixture, lax.rem(zi + hop, NZ), 0, keepdims=False)
        total += fetch(block, -hop).astype(jnp.float32)
    return total.astype(jnp.bfloat16)


def solution(mesh):
    fine = Mesh(mesh.devices.reshape(SIZES), FINE)
    both = EXPERT + TENSOR
    return jax.shard_map(
        on_device,
        mesh=fine,
        in_specs=(
            P(EXPERT, TENSOR),
            P(TENSOR, EXPERT),
            P(),
            P(both, None),
            P(both, None),
            P(both, None, None),
            P(both, None, None),
            P(both, None, None),
        ),
        out_specs=P(both, None),
        check_vma=False,
    )
```

```python
import functools

import jax
import jax.numpy as jnp
from jax import lax
from jax.experimental import pallas as pl
from jax.experimental.pallas import tpu as pltpu
from jax.sharding import Mesh
from jax.sharding import PartitionSpec as P

TOPK = 8
CAP = 2
LANES = 128
F32, BF16 = jnp.float32, jnp.bfloat16

FINE = ("z", "xl", "xh", "y", "c")
SIZES = (8, 2, 2, 4, 2)
EXPERT = ("z", "xl")
TENSOR = ("xh", "y", "c")
SPREAD = ("xh", "y")
PLANE = ("xl", "xh", "y")
NZ = 8
MIB = 1 << 20

VMEM = pl.BlockSpec(memory_space=pltpu.VMEM)
SMEM = pl.BlockSpec(memory_space=pltpu.SMEM)


def swap(x, axis):
    return lax.ppermute(x, axis, [(0, 1), (1, 0)])


def fetch(x, hop):
    return lax.ppermute(x, "z", [((i + hop) % NZ, i) for i in range(NZ)])


def gather_z(x):
    up1, dn1 = fetch(x, 1), fetch(x, -1)
    up2, dn2 = fetch(x, 2), fetch(x, -2)
    up3, dn3 = fetch(up1, 2), fetch(dn1, -2)
    far = fetch(up3, 1)
    return [x, up1, up2, up3, far, dn3, dn2, dn1]


def params(mib):
    return pltpu.CompilerParams(vmem_limit_bytes=mib * MIB)


def dot(a, b):
    return jnp.dot(a, b, preferred_element_type=F32)


def project_kernel(place, *refs):
    blocks, (own, other, give, keep, rhs, held) = refs[:NZ], refs[NZ:]
    core, xl = place[0], place[1]
    cols = own.shape[1]
    rhs[:, pl.ds(pl.multiple_of(xl * cols, LANES), cols)] = own[...]
    rhs[:, pl.ds(pl.multiple_of((1 - xl) * cols, LANES), cols)] = other[...]
    lhs = jnp.concatenate([b[...] for b in blocks], axis=0)
    total = dot(lhs, rhs[...])
    spread = give.shape[0]
    rows = lhs.shape[0] // (NZ * spread * 2)
    total = total.reshape(NZ, spread, 2, rows, 2 * cols)
    for k in range(NZ):
        at = slice(k * rows, (k + 1) * rows)
        first, second = total[k, :, 0], total[k, :, 1]
        keep[:, at, :] = jnp.where(core == 0, first, second)
        held[:, at, :] = jnp.where(core == 0, second, first)
    give[...] = held[...].astype(BF16)


def project(place, blocks, own, other, spread):
    rows = blocks[0].shape[0] // (2 * spread)
    shape = (spread, NZ * rows, 2 * own.shape[1])
    return pl.pallas_call(
        project_kernel,
        out_shape=(jax.ShapeDtypeStruct(shape, BF16), jax.ShapeDtypeStruct(shape, F32)),
        in_specs=[SMEM] + [VMEM] * (NZ + 2),
        out_specs=(VMEM, VMEM),
        scratch_shapes=[
            pltpu.VMEM((own.shape[0], 2 * own.shape[1]), BF16),
            pltpu.VMEM(shape, F32),
        ],
        compiler_params=params(32),
    )(place, *blocks, own, other)


def settle_kernel(place, parts, note, out, held):
    z = place[0]
    tokens = parts.shape[1]
    rows = tokens // NZ
    total = parts[0].astype(F32)
    for i in range(1, parts.shape[0]):
        total += parts[i].astype(F32)
    held[tokens:, :] = jnp.zeros((held.shape[0] - tokens, held.shape[1]), F32)
    held[tokens : tokens + rows, :LANES] = note[...]
    for k in range(NZ):
        at = pl.multiple_of(lax.rem(z + k, NZ) * rows, rows)
        held[pl.ds(at, rows), :] = total[k * rows : (k + 1) * rows]
    out[...] = held[...].astype(BF16)


def settle(place, parts, note):
    shape = (parts.shape[1] + 16, parts.shape[2])
    return pl.pallas_call(
        settle_kernel,
        out_shape=jax.ShapeDtypeStruct(shape, BF16),
        in_specs=[SMEM, VMEM, VMEM],
        out_specs=VMEM,
        scratch_shapes=[pltpu.VMEM(shape, F32)],
        compiler_params=params(16),
    )(place, parts, note)


def place_kernel(place, *refs):
    blocks, (gain, sent, own, high, low, stream, notes, mass) = refs[:NZ], refs[NZ:]
    z = place[0]
    tokens, width = stream.shape
    rows, wide = tokens // NZ, width // NZ
    lanes = sent.shape[0]
    for hop in range(NZ):
        there = lax.rem(z + hop, NZ)
        at = pl.multiple_of(there * wide, LANES)
        stream[:, pl.ds(at, wide)] = blocks[hop][:tokens, :].astype(F32)
        note = blocks[hop][tokens:, :LANES].astype(F32)
        notes[pl.ds(pl.multiple_of(there * rows, rows), rows), :] = note[:rows]
    own[...] = stream[pl.ds(pl.multiple_of(z * rows, rows), rows), :]

    slots = NZ * CAP
    lane = lax.broadcasted_iota(jnp.int32, (tokens, lanes), 1)
    token = lax.broadcasted_iota(jnp.int32, (tokens, lanes), 0)
    label = (z * (lanes // (2 * slots)) + lane // (2 * slots)).astype(F32)
    listed = notes[...]
    match = jnp.zeros((tokens, lanes), F32)
    gate = jnp.zeros((tokens, lanes), F32)
    for k in range(TOPK):
        hit = listed[:, k : k + 1] == label
        value = listed[:, TOPK + k : TOPK + k + 1] + listed[:, 2 * TOPK + k : 2 * TOPK + k + 1]
        match += jnp.where(hit, 1.0, 0.0)
        gate += jnp.where(hit, value, 0.0)
    before = lax.broadcasted_iota(jnp.int32, (tokens, tokens), 1)
    after = lax.broadcasted_iota(jnp.int32, (tokens, tokens), 0)
    earlier = (before // rows == after // rows) & (before < after)
    rank = dot(jnp.where(earlier, 1.0, 0.0).astype(BF16), match.astype(BF16))
    slot = (token // rows) * CAP + rank.astype(jnp.int32)
    placed = (match > 0.5) & (slot == lane % slots) & (rank < CAP - 0.5)
    mass[...] = jnp.where(placed, gate, 0.0)
    spots = jnp.transpose(jnp.where(placed, 1.0, 0.0)).astype(BF16)

    weight = jnp.concatenate(
        [
            mass[pl.ds(pl.multiple_of(lax.rem(z + hop, NZ) * rows, rows), rows), :]
            for hop in range(NZ)
        ],
        axis=0,
    )
    top = weight.astype(BF16)
    high[...] = top
    low[...] = (weight - top.astype(F32)).astype(BF16)

    square = jnp.zeros((tokens, 1), F32)
    for hop in range(NZ):
        part = stream[:, hop * wide : (hop + 1) * wide]
        square += jnp.sum(part * part, axis=-1, keepdims=True)
    scale = lax.rsqrt(square / width + 1e-06)
    for hop in range(NZ):
        at = slice(hop * wide, (hop + 1) * wide)
        normed = (stream[:, at] * scale * gain[:, at]).astype(BF16)
        sent[:, at] = dot(spots, normed).astype(BF16)


def place_rows(place, blocks, gain, plane):
    tokens = blocks[0].shape[0] - 16
    width = NZ * blocks[0].shape[1]
    rows = tokens // NZ
    lanes = plane * NZ * CAP
    return pl.pallas_call(
        place_kernel,
        out_shape=(
            jax.ShapeDtypeStruct((lanes, width), BF16),
            jax.ShapeDtypeStruct((rows, width), F32),
            jax.ShapeDtypeStruct((tokens, lanes), BF16),
            jax.ShapeDtypeStruct((tokens, lanes), BF16),
        ),
        in_specs=[SMEM] + [VMEM] * (NZ + 1),
        out_specs=(VMEM,) * 4,
        scratch_shapes=[
            pltpu.VMEM((tokens, width), F32),
            pltpu.VMEM((tokens, LANES), F32),
            pltpu.VMEM((tokens, lanes), F32),
        ],
        compiler_params=params(32),
    )(place, *blocks, gain.reshape(1, width))


def hidden_step(step, steps, rows, w_gate, w_up, gate_acc, up_acc):
    @pl.when(step == 0)
    def _():
        gate_acc[...] = dot(rows[...], w_gate[0])
        up_acc[...] = dot(rows[...], w_up[0])

    @pl.when((step > 0) & (step < steps))
    def _():
        gate_acc[...] += dot(rows[...], w_gate[0])
        up_acc[...] += dot(rows[...], w_up[0])


def hidden_of(gate_acc, up_acc):
    return (jax.nn.silu(gate_acc[...]) * up_acc[...]).astype(BF16)


def hidden_kernel(steps, rows, w_gate, w_up, out, gate_acc, up_acc):
    step = pl.program_id(0)
    hidden_step(step, steps, rows, w_gate, w_up, gate_acc, up_acc)

    @pl.when(step == steps - 1)
    def _():
        out[...] = hidden_of(gate_acc, up_acc)


def hidden_rows(rows, w_gate, w_up, steps=4):
    count, width = rows.shape
    units = w_gate.shape[2]
    deep = width // steps
    return pl.pallas_call(
        functools.partial(hidden_kernel, steps),
        grid=(steps,),
        out_shape=jax.ShapeDtypeStruct((count, units), BF16),
        in_specs=[
            pl.BlockSpec((count, deep), lambda i: (0, i)),
            pl.BlockSpec((1, deep, units), lambda i: (0, i, 0)),
            pl.BlockSpec((1, deep, units), lambda i: (0, i, 0)),
        ],
        out_specs=pl.BlockSpec((count, units), lambda i: (0, 0)),
        scratch_shapes=[pltpu.VMEM((count, units), F32)] * 2,
        compiler_params=params(32),
    )(rows, w_gate, w_up)


def expert_kernel(steps, rows, w_gate, w_up, w_down, out, gate_acc, up_acc, hidden):
    step = pl.program_id(0)
    hidden_step(step, steps, rows, w_gate, w_up, gate_acc, up_acc)

    @pl.when(step == steps)
    def _():
        hidden[...] = hidden_of(gate_acc, up_acc)

    @pl.when(step >= steps)
    def _():
        out[...] = dot(hidden[...], w_down[0]).astype(BF16)


def expert_rows(rows, w_gate, w_up, w_down, steps=4):
    count, width = rows.shape
    units = w_gate.shape[2]
    deep = width // steps
    early = lambda i: jnp.minimum(i, steps - 1)
    late = lambda i: jnp.maximum(i - steps, 0)
    return pl.pallas_call(
        functools.partial(expert_kernel, steps),
        grid=(2 * steps,),
        out_shape=jax.ShapeDtypeStruct((count, width), BF16),
        in_specs=[
            pl.BlockSpec((count, deep), lambda i: (0, early(i))),
            pl.BlockSpec((1, deep, units), lambda i: (0, early(i), 0)),
            pl.BlockSpec((1, deep, units), lambda i: (0, early(i), 0)),
            pl.BlockSpec((1, units, deep), lambda i: (0, 0, late(i))),
        ],
        out_specs=pl.BlockSpec((count, deep), lambda i: (0, late(i))),
        scratch_shapes=[pltpu.VMEM((count, units), F32)] * 2 + [pltpu.VMEM((count, units), BF16)],
        compiler_params=params(32),
    )(rows, w_gate, w_up, w_down)


def down_kernel(hidden, w_down, mate, out):
    out[...] = (dot(hidden[...], w_down[0]) + mate[...].astype(F32)).astype(BF16)


def down_rows(hidden, w_down, mate, steps=4):
    count, width = mate.shape
    units = hidden.shape[1]
    deep = width // steps
    return pl.pallas_call(
        down_kernel,
        grid=(steps,),
        out_shape=jax.ShapeDtypeStruct((count, width), BF16),
        in_specs=[
            pl.BlockSpec((count, units), lambda i: (0, 0)),
            pl.BlockSpec((1, units, deep), lambda i: (0, 0, i)),
            pl.BlockSpec((count, deep), lambda i: (0, i)),
        ],
        out_specs=pl.BlockSpec((count, deep), lambda i: (0, i)),
        compiler_params=params(32),
    )(hidden, w_down, mate)


def combine_kernel(high, low, back, own, base, *outs):
    rows, width = own.shape
    wide = width // 4
    for i in range(4):
        at = slice(i * wide, (i + 1) * wide)
        piece = back[:, at]
        mix = dot(high[...], piece) + dot(low[...], piece)
        base[:, at] = own[:, at] + mix[:rows]
        for hop in range(1, NZ):
            outs[hop - 1][:, at] = mix[hop * rows : (hop + 1) * rows].astype(BF16)


def combine(high, low, back, own):
    rows, width = own.shape
    return pl.pallas_call(
        combine_kernel,
        out_shape=(jax.ShapeDtypeStruct((rows, width), F32),)
        + (jax.ShapeDtypeStruct((rows, width), BF16),) * (NZ - 1),
        in_specs=[VMEM] * 4,
        out_specs=(VMEM,) * NZ,
        compiler_params=params(32),
    )(high, low, back, own)


def on_device(context, proj_weight, norm_gain, expert_ids, gate_values, w_gate, w_up, w_down):
    zi, xli, ci = (lax.axis_index(a).astype(jnp.int32) for a in ("z", "xl", "c"))
    n_spread = lax.axis_size(SPREAD)
    n_plane = lax.axis_size(PLANE)
    rows = expert_ids.shape[0]

    high = lax.reduce_precision(gate_values, exponent_bits=8, mantissa_bits=7)
    note = jnp.concatenate([expert_ids.astype(F32), high, gate_values - high], axis=1)
    note = jnp.pad(note, ((0, 0), (0, LANES - 3 * TOPK)))

    other = swap(proj_weight, "xl")
    give, keep = project(jnp.stack([ci, xli]), gather_z(context), proj_weight, other, n_spread)
    got = swap(give, "c")
    partial = (keep + got.astype(F32)).astype(BF16)
    partial = lax.all_to_all(partial, SPREAD, 0, 0, tiled=True)

    place = zi.reshape(1)
    part = settle(place, partial, note)
    sent, own, high, low = place_rows(place, gather_z(part), norm_gain, n_plane)
    width = sent.shape[1]
    mine = lax.all_to_all(sent.reshape(n_plane, -1, width), PLANE, 0, 0, tiled=True)
    mine = mine.reshape(-1, width)

    theirs = swap(mine, "c")
    hidden = hidden_rows(mine, w_gate, w_up)
    from_mate = swap(expert_rows(theirs, w_gate, w_up, w_down), "c")
    summed = down_rows(hidden, w_down, from_mate)
    back = lax.all_to_all(summed.reshape(n_plane, -1, width), PLANE, 0, 0, tiled=True)

    base, *blocks = combine(high, low, back.reshape(-1, width), own)
    total = base
    for hop in (4, 1, 7, 2, 6, 3, 5):
        total += fetch(blocks[hop - 1], -hop).astype(F32)
    return total.astype(BF16)


def solution(mesh):
    fine = Mesh(mesh.devices.reshape(SIZES), FINE)
    both = EXPERT + TENSOR
    return jax.shard_map(
        on_device,
        mesh=fine,
        in_specs=(
            P(EXPERT, TENSOR),
            P(TENSOR, EXPERT),
            P(),
            P(both, None),
            P(both, None),
            P(both, None, None),
            P(both, None, None),
            P(both, None, None),
        ),
        out_specs=P(both, None),
        check_vma=False,
    )
```

```python
import jax
import jax.numpy as jnp
from jax import lax
from jax.experimental import pallas as pl
from jax.experimental.pallas import tpu as pltpu
from jax.sharding import Mesh
from jax.sharding import PartitionSpec as P

TOPK = 8
CAP = 2
LANES = 128
F32, BF16 = jnp.float32, jnp.bfloat16

FINE = ("z", "xl", "xh", "y", "c")
SIZES = (8, 2, 2, 4, 2)
EXPERT = ("z", "xl")
TENSOR = ("xh", "y", "c")
SPREAD = ("xh", "y")
PLANE = ("xl", "xh", "y")
NZ = 8
MIB = 1 << 20

VMEM = pl.BlockSpec(memory_space=pltpu.VMEM)
SMEM = pl.BlockSpec(memory_space=pltpu.SMEM)


def swap(x, axis):
    return lax.ppermute(x, axis, [(0, 1), (1, 0)])


def fetch(x, hop):
    return lax.ppermute(x, "z", [((i + hop) % NZ, i) for i in range(NZ)])


def gather_z(x):
    up1, dn1 = fetch(x, 1), fetch(x, -1)
    up2, dn2 = fetch(x, 2), fetch(x, -2)
    up3, dn3 = fetch(up1, 2), fetch(dn1, -2)
    far = fetch(up3, 1)
    return [x, up1, up2, up3, far, dn3, dn2, dn1]


def params(mib):
    return pltpu.CompilerParams(vmem_limit_bytes=mib * MIB)


def dot(a, b):
    return jnp.dot(a, b, preferred_element_type=F32)


def stage_kernel(place, own, other, context, rhs, held):
    xl = place[1]
    cols = own.shape[1]
    rhs[:, pl.ds(pl.multiple_of(xl * cols, LANES), cols)] = own[...]
    rhs[:, pl.ds(pl.multiple_of((1 - xl) * cols, LANES), cols)] = other[...]
    held[...] = context[...]


def stage(place, own, other, context):
    return pl.pallas_call(
        stage_kernel,
        out_shape=(
            jax.ShapeDtypeStruct((own.shape[0], 2 * own.shape[1]), BF16),
            jax.ShapeDtypeStruct(context.shape, BF16),
        ),
        in_specs=[SMEM] + [VMEM] * 3,
        out_specs=(VMEM, VMEM),
        compiler_params=params(16),
    )(place, own, other, context)


def project_kernel(place, *refs):
    blocks, (rhs, give, keep, held) = refs[:NZ], refs[NZ:]
    core = place[0]
    lhs = jnp.concatenate([b[...] for b in blocks], axis=0)
    total = dot(lhs, rhs[...])
    spread = give.shape[0]
    rows = lhs.shape[0] // (NZ * spread * 2)
    total = total.reshape(NZ, spread, 2, rows, rhs.shape[1])
    for k in range(NZ):
        at = slice(k * rows, (k + 1) * rows)
        first, second = total[k, :, 0], total[k, :, 1]
        keep[:, at, :] = jnp.where(core == 0, first, second)
        held[:, at, :] = jnp.where(core == 0, second, first)
    give[...] = held[...].astype(BF16)


def project(place, blocks, rhs, spread):
    rows = blocks[0].shape[0] // (2 * spread)
    shape = (spread, NZ * rows, rhs.shape[1])
    return pl.pallas_call(
        project_kernel,
        out_shape=(jax.ShapeDtypeStruct(shape, BF16), jax.ShapeDtypeStruct(shape, F32)),
        in_specs=[SMEM] + [VMEM] * (NZ + 1),
        out_specs=(VMEM, VMEM),
        scratch_shapes=[pltpu.VMEM(shape, F32)],
        compiler_params=params(32),
    )(place, *blocks, rhs)


def settle_kernel(place, parts, note, out, held):
    z = place[0]
    tokens = parts.shape[1]
    rows = tokens // NZ
    total = parts[0].astype(F32)
    for i in range(1, parts.shape[0]):
        total += parts[i].astype(F32)
    held[tokens:, :] = jnp.zeros((held.shape[0] - tokens, held.shape[1]), F32)
    held[tokens : tokens + rows, :LANES] = note[...]
    for k in range(NZ):
        at = pl.multiple_of(lax.rem(z + k, NZ) * rows, rows)
        held[pl.ds(at, rows), :] = total[k * rows : (k + 1) * rows]
    out[...] = held[...].astype(BF16)


def settle(place, parts, note):
    shape = (parts.shape[1] + 16, parts.shape[2])
    return pl.pallas_call(
        settle_kernel,
        out_shape=jax.ShapeDtypeStruct(shape, BF16),
        in_specs=[SMEM, VMEM, VMEM],
        out_specs=VMEM,
        scratch_shapes=[pltpu.VMEM(shape, F32)],
        compiler_params=params(16),
    )(place, parts, note)


def place_kernel(place, *refs):
    blocks, (gain, sent, own, high, low, stream, notes, mass) = refs[:NZ], refs[NZ:]
    z = place[0]
    tokens, width = stream.shape
    rows, wide = tokens // NZ, width // NZ
    lanes = sent.shape[0]
    for hop in range(NZ):
        there = lax.rem(z + hop, NZ)
        at = pl.multiple_of(there * wide, LANES)
        stream[:, pl.ds(at, wide)] = blocks[hop][:tokens, :].astype(F32)
        note = blocks[hop][tokens:, :LANES].astype(F32)
        notes[pl.ds(pl.multiple_of(there * rows, rows), rows), :] = note[:rows]
    own[...] = stream[pl.ds(pl.multiple_of(z * rows, rows), rows), :]

    slots = NZ * CAP
    lane = lax.broadcasted_iota(jnp.int32, (tokens, lanes), 1)
    token = lax.broadcasted_iota(jnp.int32, (tokens, lanes), 0)
    label = (z * (lanes // (2 * slots)) + lane // (2 * slots)).astype(F32)
    listed = notes[...]
    match = jnp.zeros((tokens, lanes), F32)
    gate = jnp.zeros((tokens, lanes), F32)
    for k in range(TOPK):
        hit = listed[:, k : k + 1] == label
        value = listed[:, TOPK + k : TOPK + k + 1] + listed[:, 2 * TOPK + k : 2 * TOPK + k + 1]
        match += jnp.where(hit, 1.0, 0.0)
        gate += jnp.where(hit, value, 0.0)
    before = lax.broadcasted_iota(jnp.int32, (tokens, tokens), 1)
    after = lax.broadcasted_iota(jnp.int32, (tokens, tokens), 0)
    earlier = (before // rows == after // rows) & (before < after)
    rank = dot(jnp.where(earlier, 1.0, 0.0).astype(BF16), match.astype(BF16))
    slot = (token // rows) * CAP + rank.astype(jnp.int32)
    placed = (match > 0.5) & (slot == lane % slots) & (rank < CAP - 0.5)
    mass[...] = jnp.where(placed, gate, 0.0)
    spots = jnp.transpose(jnp.where(placed, 1.0, 0.0)).astype(BF16)

    weight = jnp.concatenate(
        [
            mass[pl.ds(pl.multiple_of(lax.rem(z + hop, NZ) * rows, rows), rows), :]
            for hop in range(NZ)
        ],
        axis=0,
    )
    top = weight.astype(BF16)
    high[...] = top
    low[...] = (weight - top.astype(F32)).astype(BF16)

    square = jnp.zeros((tokens, 1), F32)
    for hop in range(NZ):
        part = stream[:, hop * wide : (hop + 1) * wide]
        square += jnp.sum(part * part, axis=-1, keepdims=True)
    scale = lax.rsqrt(square / width + 1e-06)
    for hop in range(NZ):
        at = slice(hop * wide, (hop + 1) * wide)
        normed = (stream[:, at] * scale * gain[:, at]).astype(BF16)
        sent[:, at] = dot(spots, normed).astype(BF16)


def place_rows(place, blocks, gain, plane):
    tokens = blocks[0].shape[0] - 16
    width = NZ * blocks[0].shape[1]
    rows = tokens // NZ
    lanes = plane * NZ * CAP
    return pl.pallas_call(
        place_kernel,
        out_shape=(
            jax.ShapeDtypeStruct((lanes, width), BF16),
            jax.ShapeDtypeStruct((rows, width), F32),
            jax.ShapeDtypeStruct((tokens, lanes), BF16),
            jax.ShapeDtypeStruct((tokens, lanes), BF16),
        ),
        in_specs=[SMEM] + [VMEM] * (NZ + 1),
        out_specs=(VMEM,) * 4,
        scratch_shapes=[
            pltpu.VMEM((tokens, width), F32),
            pltpu.VMEM((tokens, LANES), F32),
            pltpu.VMEM((tokens, lanes), F32),
        ],
        compiler_params=params(32),
    )(place, *blocks, gain.reshape(1, width))


def expert_kernel(rows, w_gate, w_up, w_down, out):
    width = rows.shape[1]
    deep = width // 4
    gate_act = up_act = 0.0
    for i in range(4):
        at = slice(i * deep, (i + 1) * deep)
        piece = rows[:, at]
        gate_act += dot(piece, w_gate[0, at, :])
        up_act += dot(piece, w_up[0, at, :])
    hidden = (jax.nn.silu(gate_act) * up_act).astype(BF16)
    for i in range(4):
        at = slice(i * deep, (i + 1) * deep)
        out[:, at] = dot(hidden, w_down[0, :, at]).astype(BF16)


def expert_rows(rows, w_gate, w_up, w_down):
    return pl.pallas_call(
        expert_kernel,
        out_shape=jax.ShapeDtypeStruct(rows.shape, BF16),
        in_specs=[VMEM] * 4,
        out_specs=VMEM,
        compiler_params=params(32),
    )(rows, w_gate, w_up, w_down)


def combine_kernel(high, low, back, own, base, *outs):
    rows, width = own.shape
    wide = width // 4
    for i in range(4):
        at = slice(i * wide, (i + 1) * wide)
        piece = back[:, at]
        mix = dot(high[...], piece) + dot(low[...], piece)
        base[:, at] = own[:, at] + mix[:rows]
        for hop in range(1, NZ):
            outs[hop - 1][:, at] = mix[hop * rows : (hop + 1) * rows].astype(BF16)


def combine(high, low, back, own):
    rows, width = own.shape
    return pl.pallas_call(
        combine_kernel,
        out_shape=(jax.ShapeDtypeStruct((rows, width), F32),)
        + (jax.ShapeDtypeStruct((rows, width), BF16),) * (NZ - 1),
        in_specs=[VMEM] * 4,
        out_specs=(VMEM,) * NZ,
        compiler_params=params(32),
    )(high, low, back, own)


def on_device(context, proj_weight, norm_gain, expert_ids, gate_values, w_gate, w_up, w_down):
    zi, xli, ci = (lax.axis_index(a).astype(jnp.int32) for a in ("z", "xl", "c"))
    n_spread = lax.axis_size(SPREAD)
    n_plane = lax.axis_size(PLANE)
    rows = expert_ids.shape[0]

    high = lax.reduce_precision(gate_values, exponent_bits=8, mantissa_bits=7)
    note = jnp.concatenate([expert_ids.astype(F32), high, gate_values - high], axis=1)
    note = jnp.pad(note, ((0, 0), (0, LANES - 3 * TOPK)))

    spot = jnp.stack([ci, xli])
    rhs, held = stage(spot, proj_weight, swap(proj_weight, "xl"), context)
    give, keep = project(spot, [held] + gather_z(context)[1:], rhs, n_spread)
    got = swap(give, "c")
    partial = (keep + got.astype(F32)).astype(BF16)
    partial, note = lax.optimization_barrier((partial, note))
    partial = lax.all_to_all(partial, SPREAD, 0, 0, tiled=True)

    place = zi.reshape(1)
    part = settle(place, partial, note)
    sent, own, high, low = place_rows(place, gather_z(part), norm_gain, n_plane)
    width = sent.shape[1]
    mine = lax.all_to_all(sent.reshape(n_plane, -1, width), PLANE, 0, 0, tiled=True)
    mine = mine.reshape(-1, width)

    theirs = swap(mine, "c")
    mine_out = expert_rows(mine, w_gate, w_up, w_down)
    from_mate = swap(expert_rows(theirs, w_gate, w_up, w_down), "c")
    summed = (mine_out.astype(F32) + from_mate.astype(F32)).astype(BF16)
    back = lax.all_to_all(summed.reshape(n_plane, -1, width), PLANE, 0, 0, tiled=True)

    base, *blocks = combine(high, low, back.reshape(-1, width), own)
    total = base
    for hop in (4, 1, 7, 2, 6, 3, 5):
        total += fetch(blocks[hop - 1], -hop).astype(F32)
    return total.astype(BF16)


def solution(mesh):
    fine = Mesh(mesh.devices.reshape(SIZES), FINE)
    both = EXPERT + TENSOR
    return jax.shard_map(
        on_device,
        mesh=fine,
        in_specs=(
            P(EXPERT, TENSOR),
            P(TENSOR, EXPERT),
            P(),
            P(both, None),
            P(both, None),
            P(both, None, None),
            P(both, None, None),
            P(both, None, None),
        ),
        out_specs=P(both, None),
        check_vma=False,
    )
```

```python
import functools

import jax
import jax.numpy as jnp
from jax import lax
from jax.experimental import pallas as pl
from jax.experimental.pallas import tpu as pltpu
from jax.sharding import Mesh
from jax.sharding import PartitionSpec as P

TOPK = 8
CAP = 2
LANES = 128
F32, BF16 = jnp.float32, jnp.bfloat16

FINE = ("z", "xl", "xh", "y", "c")
SIZES = (8, 2, 2, 4, 2)
EXPERT = ("z", "xl")
TENSOR = ("xh", "y", "c")
SPREAD = ("xh", "y")
PLANE = ("xl", "xh", "y")
NZ = 8
MIB = 1 << 20

VMEM = pl.BlockSpec(memory_space=pltpu.VMEM)
SMEM = pl.BlockSpec(memory_space=pltpu.SMEM)


def swap(x, axis):
    return lax.ppermute(x, axis, [(0, 1), (1, 0)])


def fetch(x, hop):
    return lax.ppermute(x, "z", [((i + hop) % NZ, i) for i in range(NZ)])


def gather_z(x):
    up2, dn2 = fetch(x, 2), fetch(x, -2)
    up1, dn1 = fetch(x, 1), fetch(x, -1)
    up3, dn3 = fetch(up2, 1), fetch(dn2, -1)
    far = fetch(up2, 2)
    return [x, up1, up2, up3, far, dn3, dn2, dn1]


def params(mib):
    return pltpu.CompilerParams(vmem_limit_bytes=mib * MIB)


def dot(a, b):
    return jnp.dot(a, b, preferred_element_type=F32)


def stage_kernel(place, own, other, context, rhs, held):
    xl = place[0]
    cols = own.shape[1]
    rhs[:, pl.ds(pl.multiple_of(xl * cols, LANES), cols)] = own[...]
    rhs[:, pl.ds(pl.multiple_of((1 - xl) * cols, LANES), cols)] = other[...]
    held[...] = context[...]


def stage(place, own, other, context):
    return pl.pallas_call(
        stage_kernel,
        out_shape=(
            jax.ShapeDtypeStruct((own.shape[0], 2 * own.shape[1]), BF16),
            jax.ShapeDtypeStruct(context.shape, BF16),
        ),
        in_specs=[SMEM] + [VMEM] * 3,
        out_specs=(VMEM, VMEM),
        compiler_params=params(16),
    )(place, own, other, context)


def project_kernel(*refs):
    blocks, (rhs, out, held) = refs[:NZ], refs[NZ:]
    lhs = jnp.concatenate([b[...] for b in blocks], axis=0)
    total = dot(lhs, rhs[...])
    peers = out.shape[0]
    rows = out.shape[1] // NZ
    total = total.reshape(NZ, peers, rows, rhs.shape[1])
    for k in range(NZ):
        held[:, k * rows : (k + 1) * rows, :] = total[k]
    out[...] = held[...].astype(BF16)


def project(blocks, rhs, peers):
    rows = blocks[0].shape[0] // peers
    shape = (peers, NZ * rows, rhs.shape[1])
    return pl.pallas_call(
        project_kernel,
        out_shape=jax.ShapeDtypeStruct(shape, BF16),
        in_specs=[VMEM] * (NZ + 1),
        out_specs=VMEM,
        scratch_shapes=[pltpu.VMEM(shape, F32)],
        compiler_params=params(32),
    )(*blocks, rhs)


def settle_kernel(place, parts, note, out, held):
    z = place[0]
    tokens = parts.shape[1]
    rows = tokens // NZ
    total = parts[0].astype(F32)
    for i in range(1, parts.shape[0]):
        total += parts[i].astype(F32)
    held[tokens:, :] = jnp.zeros((held.shape[0] - tokens, held.shape[1]), F32)
    held[tokens : tokens + rows, :LANES] = note[...]
    for k in range(NZ):
        at = pl.multiple_of(lax.rem(z + k, NZ) * rows, rows)
        held[pl.ds(at, rows), :] = total[k * rows : (k + 1) * rows]
    out[...] = held[...].astype(BF16)


def settle(place, parts, note):
    shape = (parts.shape[1] + 16, parts.shape[2])
    return pl.pallas_call(
        settle_kernel,
        out_shape=jax.ShapeDtypeStruct(shape, BF16),
        in_specs=[SMEM, VMEM, VMEM],
        out_specs=VMEM,
        scratch_shapes=[pltpu.VMEM(shape, F32)],
        compiler_params=params(16),
    )(place, parts, note)


def place_kernel(place, *refs):
    blocks, (gain, sent, own, high, low, stream, notes) = refs[:NZ], refs[NZ:]
    z = place[0]
    tokens, width = stream.shape
    rows, wide = tokens // NZ, width // NZ
    lanes = sent.shape[0]
    for hop in range(NZ):
        there = lax.rem(z + hop, NZ)
        at = pl.multiple_of(there * wide, LANES)
        stream[:, pl.ds(at, wide)] = blocks[hop][:tokens, :].astype(F32)
        note = blocks[hop][tokens:, :LANES].astype(F32)
        notes[pl.ds(pl.multiple_of(there * rows, rows), rows), :] = note[:rows]
    own[...] = stream[pl.ds(pl.multiple_of(z * rows, rows), rows), :]

    slots = NZ * CAP
    lane = lax.broadcasted_iota(jnp.int32, (tokens, lanes), 1)
    token = lax.broadcasted_iota(jnp.int32, (tokens, lanes), 0)
    label = (z * (lanes // (2 * slots)) + lane // (2 * slots)).astype(F32)
    listed = notes[...]
    match = jnp.zeros((tokens, lanes), F32)
    gate = jnp.zeros((tokens, lanes), F32)
    for k in range(TOPK):
        hit = listed[:, k : k + 1] == label
        value = listed[:, TOPK + k : TOPK + k + 1] + listed[:, 2 * TOPK + k : 2 * TOPK + k + 1]
        match += jnp.where(hit, 1.0, 0.0)
        gate += jnp.where(hit, value, 0.0)
    before = lax.broadcasted_iota(jnp.int32, (tokens, tokens), 1)
    after = lax.broadcasted_iota(jnp.int32, (tokens, tokens), 0)
    earlier = (before // rows == after // rows) & (before < after)
    rank = dot(jnp.where(earlier, 1.0, 0.0).astype(BF16), match.astype(BF16))
    slot = (token // rows) * CAP + rank.astype(jnp.int32)
    placed = (match > 0.5) & (slot == lane % slots) & (rank < CAP - 0.5)
    spots = jnp.transpose(jnp.where(placed, 1.0, 0.0)).astype(BF16)

    weight = jnp.where(placed, gate, 0.0)
    top = weight.astype(BF16)
    high[...] = top
    low[...] = (weight - top.astype(F32)).astype(BF16)

    square = jnp.zeros((tokens, 1), F32)
    for hop in range(NZ):
        part = stream[:, hop * wide : (hop + 1) * wide]
        square += jnp.sum(part * part, axis=-1, keepdims=True)
    scale = lax.rsqrt(square / width + 1e-06)
    for hop in range(NZ):
        at = slice(hop * wide, (hop + 1) * wide)
        normed = (stream[:, at] * scale * gain[:, at]).astype(BF16)
        sent[:, at] = dot(spots, normed).astype(BF16)


def place_rows(place, blocks, gain, plane):
    tokens = blocks[0].shape[0] - 16
    width = NZ * blocks[0].shape[1]
    rows = tokens // NZ
    lanes = plane * NZ * CAP
    return pl.pallas_call(
        place_kernel,
        out_shape=(
            jax.ShapeDtypeStruct((lanes, width), BF16),
            jax.ShapeDtypeStruct((rows, width), F32),
            jax.ShapeDtypeStruct((tokens, lanes), BF16),
            jax.ShapeDtypeStruct((tokens, lanes), BF16),
        ),
        in_specs=[SMEM] + [VMEM] * (NZ + 1),
        out_specs=(VMEM,) * 4,
        scratch_shapes=[
            pltpu.VMEM((tokens, width), F32),
            pltpu.VMEM((tokens, LANES), F32),
        ],
        compiler_params=params(32),
    )(place, *blocks, gain.reshape(1, width))


def expert_kernel(first, rows, w_gate, w_up, w_down, out, down, arrived):
    copy = pltpu.make_async_copy(w_down, down, arrived)
    copy.start()
    count, width = out.shape
    deep = width // 4
    gate_act = up_act = 0.0
    for i in range(4):
        at = slice(i * deep, (i + 1) * deep)
        piece = rows[first : first + count, at]
        gate_act += dot(piece, w_gate[0, at, :])
        up_act += dot(piece, w_up[0, at, :])
    hidden = (jax.nn.silu(gate_act) * up_act).astype(BF16)
    copy.wait()
    for i in range(4):
        at = slice(i * deep, (i + 1) * deep)
        out[:, at] = dot(hidden, down[0, :, at]).astype(BF16)


def expert_rows(rows, first, count, w_gate, w_up, w_down):
    return pl.pallas_call(
        functools.partial(expert_kernel, first),
        out_shape=jax.ShapeDtypeStruct((count, rows.shape[1]), BF16),
        in_specs=[VMEM] * 3 + [pl.BlockSpec(memory_space=pl.ANY)],
        out_specs=VMEM,
        scratch_shapes=[pltpu.VMEM(w_down.shape, BF16), pltpu.SemaphoreType.DMA],
        compiler_params=params(32),
    )(rows, w_gate, w_up, w_down)


def add_kernel(mine, *refs):
    parts, out = refs[:-1], refs[-1]
    count = parts[0].shape[0]
    for i, part in enumerate(parts):
        at = slice(i * count, (i + 1) * count)
        out[at, :] = (mine[at, :].astype(F32) + part[...].astype(F32)).astype(BF16)


def add_rows(mine, parts):
    return pl.pallas_call(
        add_kernel,
        out_shape=jax.ShapeDtypeStruct(mine.shape, BF16),
        in_specs=[VMEM] * (1 + len(parts)),
        out_specs=VMEM,
        compiler_params=params(32),
    )(mine, *parts)


def combine_kernel(high, low, back, out):
    width = back.shape[1]
    wide = width // 4
    for i in range(4):
        at = slice(i * wide, (i + 1) * wide)
        piece = back[:, at]
        out[:, at] = (dot(high[...], piece) + dot(low[...], piece)).astype(BF16)


def combine(high, low, back):
    return pl.pallas_call(
        combine_kernel,
        out_shape=jax.ShapeDtypeStruct((high.shape[0], back.shape[1]), BF16),
        in_specs=[VMEM] * 3,
        out_specs=VMEM,
        compiler_params=params(32),
    )(high, low, back)


def on_device(context, proj_weight, norm_gain, expert_ids, gate_values, w_gate, w_up, w_down):
    zi, xli = (lax.axis_index(a).astype(jnp.int32) for a in ("z", "xl"))
    n_tensor = lax.axis_size(TENSOR)
    n_plane = lax.axis_size(PLANE)

    high = lax.reduce_precision(gate_values, exponent_bits=8, mantissa_bits=7)
    note = jnp.concatenate([expert_ids.astype(F32), high, gate_values - high], axis=1)
    note = jnp.pad(note, ((0, 0), (0, LANES - 3 * TOPK)))

    place = zi.reshape(1)
    rhs, held = stage(xli.reshape(1), proj_weight, swap(proj_weight, "xl"), context)
    partial = project([held] + gather_z(context)[1:], rhs, n_tensor)
    partial, note, place = lax.optimization_barrier((partial, note, place))
    partial = lax.all_to_all(partial, TENSOR, 0, 0, tiled=True)

    part = settle(place, partial, note)
    sent, own, high, low = place_rows(place, gather_z(part), norm_gain, n_plane)
    width = sent.shape[1]
    mine = lax.all_to_all(sent.reshape(n_plane, -1, width), PLANE, 0, 0, tiled=True)
    mine = mine.reshape(-1, width)

    weights = (w_gate, w_up, w_down)
    theirs = swap(mine, "c")
    count = mine.shape[0]
    mine_out = expert_rows(mine, 0, count, *weights)
    theirs, mine_out = lax.optimization_barrier((theirs, mine_out))
    half = count // 2
    parts = [swap(expert_rows(theirs, at, half, *weights), "c") for at in (0, half)]
    summed = add_rows(mine_out, parts).reshape(n_plane, -1, width)
    back = lax.all_to_all(summed, PLANE, 0, 0, tiled=True).reshape(-1, width)

    mixture = combine(high, low, back).reshape(NZ, -1, width)
    home = lax.all_to_all(mixture, "z", 0, 0, tiled=True)
    return (own + jnp.sum(home.astype(F32), axis=0)).astype(BF16)


def solution(mesh):
    fine = Mesh(mesh.devices.reshape(SIZES), FINE)
    both = EXPERT + TENSOR
    return jax.shard_map(
        on_device,
        mesh=fine,
        in_specs=(
            P(EXPERT, TENSOR),
            P(TENSOR, EXPERT),
            P(),
            P(both, None),
            P(both, None),
            P(both, None, None),
            P(both, None, None),
            P(both, None, None),
        ),
        out_specs=P(both, None),
        check_vma=False,
    )
```

```python
import functools

import jax
import jax.numpy as jnp
from jax import lax
from jax.experimental import pallas as pl
from jax.experimental.pallas import tpu as pltpu
from jax.sharding import Mesh
from jax.sharding import PartitionSpec as P

TOPK = 8
CAP = 2
LANES = 128
F32, BF16 = jnp.float32, jnp.bfloat16

FINE = ("z", "xl", "xh", "y", "c")
SIZES = (8, 2, 2, 4, 2)
EXPERT = ("z", "xl")
TENSOR = ("xh", "y", "c")
SPREAD = ("xh", "y")
PLANE = ("xl", "xh", "y")
NZ = 8
MIB = 1 << 20

VMEM = pl.BlockSpec(memory_space=pltpu.VMEM)
SMEM = pl.BlockSpec(memory_space=pltpu.SMEM)


def swap(x, axis):
    return lax.ppermute(x, axis, [(0, 1), (1, 0)])


def fetch(x, hop):
    return lax.ppermute(x, "z", [((i + hop) % NZ, i) for i in range(NZ)])


def gather_z(x):
    up2, dn2 = fetch(x, 2), fetch(x, -2)
    up1, dn1 = fetch(x, 1), fetch(x, -1)
    up3, dn3 = fetch(up2, 1), fetch(dn2, -1)
    far = fetch(up2, 2)
    return [x, up1, up2, up3, far, dn3, dn2, dn1]


def params(mib):
    return pltpu.CompilerParams(vmem_limit_bytes=mib * MIB)


def dot(a, b):
    return jnp.dot(a, b, preferred_element_type=F32)


def stage_kernel(place, own, other, context, rhs, held):
    xl = place[0]
    cols = own.shape[1]
    rhs[:, pl.ds(pl.multiple_of(xl * cols, LANES), cols)] = own[...]
    rhs[:, pl.ds(pl.multiple_of((1 - xl) * cols, LANES), cols)] = other[...]
    held[...] = context[...]


def stage(place, own, other, context):
    return pl.pallas_call(
        stage_kernel,
        out_shape=(
            jax.ShapeDtypeStruct((own.shape[0], 2 * own.shape[1]), BF16),
            jax.ShapeDtypeStruct(context.shape, BF16),
        ),
        in_specs=[SMEM] + [VMEM] * 3,
        out_specs=(VMEM, VMEM),
        compiler_params=params(16),
    )(place, own, other, context)


def project_kernel(place, *refs):
    blocks, (rhs, give, keep, held) = refs[:NZ], refs[NZ:]
    core = place[1]
    lhs = jnp.concatenate([b[...] for b in blocks], axis=0)
    total = dot(lhs, rhs[...])
    spread = give.shape[0]
    rows = give.shape[1] // NZ
    total = total.reshape(NZ, spread, 2, rows, rhs.shape[1])
    for k in range(NZ):
        at = slice(k * rows, (k + 1) * rows)
        first, second = total[k, :, 0], total[k, :, 1]
        keep[:, at, :] = jnp.where(core == 0, first, second)
        held[:, at, :] = jnp.where(core == 0, second, first)
    give[...] = held[...].astype(BF16)


def project(place, blocks, rhs, spread):
    rows = blocks[0].shape[0] // (2 * spread)
    shape = (spread, NZ * rows, rhs.shape[1])
    return pl.pallas_call(
        project_kernel,
        out_shape=(jax.ShapeDtypeStruct(shape, BF16), jax.ShapeDtypeStruct(shape, F32)),
        in_specs=[SMEM] + [VMEM] * (NZ + 1),
        out_specs=(VMEM, VMEM),
        scratch_shapes=[pltpu.VMEM(shape, F32)],
        compiler_params=params(32),
    )(place, *blocks, rhs)


def join_kernel(keep, got, out):
    out[...] = (keep[...] + got[...].astype(F32)).astype(BF16)


def join(keep, got):
    return pl.pallas_call(
        join_kernel,
        out_shape=jax.ShapeDtypeStruct(keep.shape, BF16),
        in_specs=[VMEM] * 2,
        out_specs=VMEM,
        compiler_params=params(16),
    )(keep, got)


def settle_kernel(place, parts, note, out, held):
    z = place[0]
    tokens = parts.shape[1]
    rows = tokens // NZ
    total = parts[0].astype(F32)
    for i in range(1, parts.shape[0]):
        total += parts[i].astype(F32)
    held[tokens:, :] = jnp.zeros((held.shape[0] - tokens, held.shape[1]), F32)
    held[tokens : tokens + rows, :LANES] = note[...]
    for k in range(NZ):
        at = pl.multiple_of(lax.rem(z + k, NZ) * rows, rows)
        held[pl.ds(at, rows), :] = total[k * rows : (k + 1) * rows]
    out[...] = held[...].astype(BF16)


def settle(place, parts, note):
    shape = (parts.shape[1] + 16, parts.shape[2])
    return pl.pallas_call(
        settle_kernel,
        out_shape=jax.ShapeDtypeStruct(shape, BF16),
        in_specs=[SMEM, VMEM, VMEM],
        out_specs=VMEM,
        scratch_shapes=[pltpu.VMEM(shape, F32)],
        compiler_params=params(16),
    )(place, parts, note)


def place_kernel(place, *refs):
    blocks, (gain, sent, own, high, low, stream, notes, mass) = refs[:NZ], refs[NZ:]
    z = place[0]
    tokens, width = stream.shape
    rows, wide = tokens // NZ, width // NZ
    lanes = sent.shape[0]
    for hop in range(NZ):
        there = lax.rem(z + hop, NZ)
        at = pl.multiple_of(there * wide, LANES)
        stream[:, pl.ds(at, wide)] = blocks[hop][:tokens, :].astype(F32)
        note = blocks[hop][tokens:, :LANES].astype(F32)
        notes[pl.ds(pl.multiple_of(there * rows, rows), rows), :] = note[:rows]
    own[...] = stream[pl.ds(pl.multiple_of(z * rows, rows), rows), :]

    slots = NZ * CAP
    lane = lax.broadcasted_iota(jnp.int32, (tokens, lanes), 1)
    token = lax.broadcasted_iota(jnp.int32, (tokens, lanes), 0)
    label = (z * (lanes // (2 * slots)) + lane // (2 * slots)).astype(F32)
    listed = notes[...]
    match = jnp.zeros((tokens, lanes), F32)
    gate = jnp.zeros((tokens, lanes), F32)
    for k in range(TOPK):
        hit = listed[:, k : k + 1] == label
        value = listed[:, TOPK + k : TOPK + k + 1] + listed[:, 2 * TOPK + k : 2 * TOPK + k + 1]
        match += jnp.where(hit, 1.0, 0.0)
        gate += jnp.where(hit, value, 0.0)
    before = lax.broadcasted_iota(jnp.int32, (tokens, tokens), 1)
    after = lax.broadcasted_iota(jnp.int32, (tokens, tokens), 0)
    earlier = (before // rows == after // rows) & (before < after)
    rank = dot(jnp.where(earlier, 1.0, 0.0).astype(BF16), match.astype(BF16))
    slot = (token // rows) * CAP + rank.astype(jnp.int32)
    placed = (match > 0.5) & (slot == lane % slots) & (rank < CAP - 0.5)
    spots = jnp.transpose(jnp.where(placed, 1.0, 0.0)).astype(BF16)

    mass[...] = jnp.where(placed, gate, 0.0)

    weight = jnp.concatenate(
        [
            mass[pl.ds(pl.multiple_of(lax.rem(z + hop, NZ) * rows, rows), rows), :]
            for hop in range(NZ)
        ],
        axis=0,
    )
    top = weight.astype(BF16)
    high[...] = top
    low[...] = (weight - top.astype(F32)).astype(BF16)

    square = jnp.zeros((tokens, 1), F32)
    for hop in range(NZ):
        part = stream[:, hop * wide : (hop + 1) * wide]
        square += jnp.sum(part * part, axis=-1, keepdims=True)
    scale = lax.rsqrt(square / width + 1e-06)
    for hop in range(NZ):
        at = slice(hop * wide, (hop + 1) * wide)
        normed = (stream[:, at] * scale * gain[:, at]).astype(BF16)
        sent[:, at] = dot(spots, normed).astype(BF16)


def place_rows(place, blocks, gain, plane):
    tokens = blocks[0].shape[0] - 16
    width = NZ * blocks[0].shape[1]
    rows = tokens // NZ
    lanes = plane * NZ * CAP
    return pl.pallas_call(
        place_kernel,
        out_shape=(
            jax.ShapeDtypeStruct((lanes, width), BF16),
            jax.ShapeDtypeStruct((rows, width), F32),
            jax.ShapeDtypeStruct((tokens, lanes), BF16),
            jax.ShapeDtypeStruct((tokens, lanes), BF16),
        ),
        in_specs=[SMEM] + [VMEM] * (NZ + 1),
        out_specs=(VMEM,) * 4,
        scratch_shapes=[
            pltpu.VMEM((tokens, width), F32),
            pltpu.VMEM((tokens, LANES), F32),
            pltpu.VMEM((tokens, lanes), F32),
        ],
        compiler_params=params(32),
    )(place, *blocks, gain.reshape(1, width))


def expert_kernel(first, rows, w_gate, w_up, w_down, out, down, arrived):
    copy = pltpu.make_async_copy(w_down, down, arrived)
    copy.start()
    count, width = out.shape
    deep = width // 4
    gate_act = up_act = 0.0
    for i in range(4):
        at = slice(i * deep, (i + 1) * deep)
        piece = rows[first : first + count, at]
        gate_act += dot(piece, w_gate[0, at, :])
        up_act += dot(piece, w_up[0, at, :])
    hidden = (jax.nn.silu(gate_act) * up_act).astype(BF16)
    copy.wait()
    for i in range(4):
        at = slice(i * deep, (i + 1) * deep)
        out[:, at] = dot(hidden, down[0, :, at]).astype(BF16)


def expert_rows(rows, first, count, w_gate, w_up, w_down):
    return pl.pallas_call(
        functools.partial(expert_kernel, first),
        out_shape=jax.ShapeDtypeStruct((count, rows.shape[1]), BF16),
        in_specs=[VMEM] * 3 + [pl.BlockSpec(memory_space=pl.ANY)],
        out_specs=VMEM,
        scratch_shapes=[pltpu.VMEM(w_down.shape, BF16), pltpu.SemaphoreType.DMA],
        compiler_params=params(32),
        cost_estimate=pl.CostEstimate(
            flops=6 * count * w_down.shape[1] * w_down.shape[2],
            bytes_accessed=6 * w_down.size + 4 * count * rows.shape[1],
            transcendentals=count * w_down.shape[1],
        ),
    )(rows, w_gate, w_up, w_down)


def add_kernel(mine, *refs):
    parts, out = refs[:-1], refs[-1]
    count = parts[0].shape[0]
    for i, part in enumerate(parts):
        at = slice(i * count, (i + 1) * count)
        out[at, :] = (mine[at, :].astype(F32) + part[...].astype(F32)).astype(BF16)


def add_rows(mine, parts):
    return pl.pallas_call(
        add_kernel,
        out_shape=jax.ShapeDtypeStruct(mine.shape, BF16),
        in_specs=[VMEM] * (1 + len(parts)),
        out_specs=VMEM,
        compiler_params=params(32),
    )(mine, *parts)


def combine_kernel(high, low, back, own, base, *outs):
    rows, width = own.shape
    wide = width // 4
    for i in range(4):
        at = slice(i * wide, (i + 1) * wide)
        piece = back[:, at]
        mix = dot(high[...], piece) + dot(low[...], piece)
        base[:, at] = own[:, at] + mix[:rows]
        for hop in range(1, NZ):
            outs[hop - 1][:, at] = mix[hop * rows : (hop + 1) * rows].astype(BF16)


def combine(high, low, back, own):
    rows, width = own.shape
    return pl.pallas_call(
        combine_kernel,
        out_shape=(jax.ShapeDtypeStruct((rows, width), F32),)
        + (jax.ShapeDtypeStruct((rows, width), BF16),) * (NZ - 1),
        in_specs=[VMEM] * 4,
        out_specs=(VMEM,) * NZ,
        compiler_params=params(32),
    )(high, low, back, own)


def on_device(context, proj_weight, norm_gain, expert_ids, gate_values, w_gate, w_up, w_down):
    zi, xli, ci = (lax.axis_index(a).astype(jnp.int32) for a in ("z", "xl", "c"))
    n_spread = lax.axis_size(SPREAD)
    n_plane = lax.axis_size(PLANE)

    high = lax.reduce_precision(gate_values, exponent_bits=8, mantissa_bits=7)
    note = jnp.concatenate([expert_ids.astype(F32), high, gate_values - high], axis=1)
    note = jnp.pad(note, ((0, 0), (0, LANES - 3 * TOPK)))

    place = zi.reshape(1)
    spot = jnp.stack([xli, ci])
    rhs, held = stage(spot, proj_weight, swap(proj_weight, "xl"), context)
    give, keep = project(spot, [held] + gather_z(context)[1:], rhs, n_spread)
    partial = join(keep, swap(give, "c"))
    partial, note, place = lax.optimization_barrier((partial, note, place))
    partial = lax.all_to_all(partial, SPREAD, 0, 0, tiled=True)

    part = settle(place, partial, note)
    sent, own, high, low = place_rows(place, gather_z(part), norm_gain, n_plane)
    width = sent.shape[1]
    mine = lax.all_to_all(sent.reshape(n_plane, -1, width), PLANE, 0, 0, tiled=True)
    mine = mine.reshape(-1, width)

    weights = (w_gate, w_up, w_down)
    theirs = swap(mine, "c")
    count = mine.shape[0]
    mine_out = expert_rows(mine, 0, count, *weights)
    theirs, mine_out = lax.optimization_barrier((theirs, mine_out))
    half = count // 2
    parts = [swap(expert_rows(theirs, at, half, *weights), "c") for at in (0, half)]
    summed = add_rows(mine_out, parts).reshape(n_plane, -1, width)
    back = lax.all_to_all(summed, PLANE, 0, 0, tiled=True).reshape(-1, width)

    total, *blocks = combine(high, low, back, own)
    for hop in (2, 6, 3, 5, 4, 1, 7):
        total += fetch(blocks[hop - 1], -hop).astype(F32)
    return total.astype(BF16)


def solution(mesh):
    fine = Mesh(mesh.devices.reshape(SIZES), FINE)
    both = EXPERT + TENSOR
    return jax.shard_map(
        on_device,
        mesh=fine,
        in_specs=(
            P(EXPERT, TENSOR),
            P(TENSOR, EXPERT),
            P(),
            P(both, None),
            P(both, None),
            P(both, None, None),
            P(both, None, None),
            P(both, None, None),
        ),
        out_specs=P(both, None),
        check_vma=False,
    )
```

```python
import functools

import jax
import jax.numpy as jnp
from jax import lax
from jax.experimental import pallas as pl
from jax.experimental.pallas import tpu as pltpu
from jax.sharding import Mesh
from jax.sharding import PartitionSpec as P

TOPK = 8
CAP = 2
LANES = 128
F32, BF16 = jnp.float32, jnp.bfloat16

FINE = ("z", "xl", "xh", "y", "c")
SIZES = (8, 2, 2, 4, 2)
EXPERT = ("z", "xl")
TENSOR = ("xh", "y", "c")
SPREAD = ("xh", "y")
PLANE = ("xl", "xh", "y")
NZ = 8
MIB = 1 << 20

VMEM = pl.BlockSpec(memory_space=pltpu.VMEM)
SMEM = pl.BlockSpec(memory_space=pltpu.SMEM)


def swap(x, axis):
    return lax.ppermute(x, axis, [(0, 1), (1, 0)])


def fetch(x, hop):
    return lax.ppermute(x, "z", [((i + hop) % NZ, i) for i in range(NZ)])


def gather_z(x):
    up2, dn2 = fetch(x, 2), fetch(x, -2)
    up1, dn1 = fetch(x, 1), fetch(x, -1)
    up3, dn3 = fetch(up2, 1), fetch(dn2, -1)
    far = fetch(up2, 2)
    return [x, up1, up2, up3, far, dn3, dn2, dn1]


def params(mib):
    return pltpu.CompilerParams(vmem_limit_bytes=mib * MIB)


def dot(a, b):
    return jnp.dot(a, b, preferred_element_type=F32)


def where(place):
    return lax.div(place[0], 4), lax.rem(lax.div(place[0], 2), 2), lax.rem(place[0], 2)


def stage_kernel(place, own, other, context, rhs, held):
    _, xl, _ = where(place)
    cols = own.shape[1]
    rhs[:, pl.ds(pl.multiple_of(xl * cols, LANES), cols)] = own[...]
    rhs[:, pl.ds(pl.multiple_of((1 - xl) * cols, LANES), cols)] = other[...]
    held[...] = context[...]


def stage(place, own, other, context):
    return pl.pallas_call(
        stage_kernel,
        out_shape=(
            jax.ShapeDtypeStruct((own.shape[0], 2 * own.shape[1]), BF16),
            jax.ShapeDtypeStruct(context.shape, BF16),
        ),
        in_specs=[SMEM] + [VMEM] * 3,
        out_specs=(VMEM, VMEM),
        compiler_params=params(16),
    )(place, own, other, context)


def project_kernel(place, *refs):
    blocks, (rhs, give, keep, held) = refs[:NZ], refs[NZ:]
    _, _, core = where(place)
    lhs = jnp.concatenate([b[...] for b in blocks], axis=0)
    total = dot(lhs, rhs[...])
    spread = give.shape[0]
    rows = give.shape[1] // NZ
    total = total.reshape(NZ, spread, 2, rows, rhs.shape[1])
    for k in range(NZ):
        at = slice(k * rows, (k + 1) * rows)
        first, second = total[k, :, 0], total[k, :, 1]
        keep[:, at, :] = jnp.where(core == 0, first, second)
        held[:, at, :] = jnp.where(core == 0, second, first)
    give[...] = held[...].astype(BF16)


def project(place, blocks, rhs, spread):
    rows = blocks[0].shape[0] // (2 * spread)
    shape = (spread, NZ * rows, rhs.shape[1])
    return pl.pallas_call(
        project_kernel,
        out_shape=(jax.ShapeDtypeStruct(shape, BF16), jax.ShapeDtypeStruct(shape, F32)),
        in_specs=[SMEM] + [VMEM] * (NZ + 1),
        out_specs=(VMEM, VMEM),
        scratch_shapes=[pltpu.VMEM(shape, F32)],
        compiler_params=params(32),
    )(place, *blocks, rhs)


def join_kernel(keep, got, out):
    out[...] = (keep[...] + got[...].astype(F32)).astype(BF16)


def join(keep, got):
    return pl.pallas_call(
        join_kernel,
        out_shape=jax.ShapeDtypeStruct(keep.shape, BF16),
        in_specs=[VMEM] * 2,
        out_specs=VMEM,
        compiler_params=params(16),
    )(keep, got)


def settle_kernel(place, parts, ids, gates, out, held):
    z, _, _ = where(place)
    tokens = parts.shape[1]
    rows = tokens // NZ
    total = parts[0].astype(F32)
    for i in range(1, parts.shape[0]):
        total += parts[i].astype(F32)
    for k in range(NZ):
        at = pl.multiple_of(lax.rem(z + k, NZ) * rows, rows)
        held[pl.ds(at, rows), :] = total[k * rows : (k + 1) * rows]
    named = ids[...].astype(F32)
    high = gates[...].astype(BF16).astype(F32)
    low = gates[...] - high
    lane = lax.broadcasted_iota(jnp.int32, (rows, held.shape[1]), 1)
    note = jnp.zeros((rows, held.shape[1]), F32)
    for i, part in enumerate((named, high, low)):
        for k in range(TOPK):
            note = jnp.where(lane == i * TOPK + k, part[:, k : k + 1], note)
    held[tokens:, :] = note
    out[...] = held[...].astype(BF16)


def settle(place, parts, ids, gates):
    shape = (parts.shape[1] + ids.shape[0], parts.shape[2])
    return pl.pallas_call(
        settle_kernel,
        out_shape=jax.ShapeDtypeStruct(shape, BF16),
        in_specs=[SMEM, VMEM, VMEM, VMEM],
        out_specs=VMEM,
        scratch_shapes=[pltpu.VMEM(shape, F32)],
        compiler_params=params(16),
    )(place, parts, ids, gates)


def place_kernel(place, *refs):
    blocks, (gain, sent, own, high, low, stream, notes, mass) = refs[:NZ], refs[NZ:]
    z, _, _ = where(place)
    tokens, width = stream.shape
    rows, wide = tokens // NZ, width // NZ
    lanes = sent.shape[0]
    for hop in range(NZ):
        there = lax.rem(z + hop, NZ)
        at = pl.multiple_of(there * wide, LANES)
        block = blocks[hop][...].astype(F32)
        stream[:, pl.ds(at, wide)] = block[:tokens]
        notes[pl.ds(pl.multiple_of(there * rows, rows), rows), :] = block[tokens:, :LANES]
    own[...] = stream[pl.ds(pl.multiple_of(z * rows, rows), rows), :]

    slots = NZ * CAP
    lane = lax.broadcasted_iota(jnp.int32, (tokens, lanes), 1)
    token = lax.broadcasted_iota(jnp.int32, (tokens, lanes), 0)
    label = (z * (lanes // (2 * slots)) + lane // (2 * slots)).astype(F32)
    listed = notes[...]
    match = jnp.zeros((tokens, lanes), F32)
    gate = jnp.zeros((tokens, lanes), F32)
    for k in range(TOPK):
        hit = listed[:, k : k + 1] == label
        value = listed[:, TOPK + k : TOPK + k + 1] + listed[:, 2 * TOPK + k : 2 * TOPK + k + 1]
        match += jnp.where(hit, 1.0, 0.0)
        gate += jnp.where(hit, value, 0.0)
    before = lax.broadcasted_iota(jnp.int32, (tokens, tokens), 1)
    after = lax.broadcasted_iota(jnp.int32, (tokens, tokens), 0)
    earlier = (before // rows == after // rows) & (before < after)
    rank = dot(jnp.where(earlier, 1.0, 0.0).astype(BF16), match.astype(BF16))
    slot = (token // rows) * CAP + rank.astype(jnp.int32)
    placed = (match > 0.5) & (slot == lane % slots) & (rank < CAP - 0.5)
    spots = jnp.transpose(jnp.where(placed, 1.0, 0.0)).astype(BF16)

    mass[...] = jnp.where(placed, gate, 0.0)

    weight = jnp.concatenate(
        [
            mass[pl.ds(pl.multiple_of(lax.rem(z + hop, NZ) * rows, rows), rows), :]
            for hop in range(NZ)
        ],
        axis=0,
    )
    top = weight.astype(BF16)
    high[...] = top
    low[...] = (weight - top.astype(F32)).astype(BF16)

    square = jnp.zeros((tokens, 1), F32)
    for hop in range(NZ):
        part = stream[:, hop * wide : (hop + 1) * wide]
        square += jnp.sum(part * part, axis=-1, keepdims=True)
    scale = lax.rsqrt(square / width + 1e-06)
    for hop in range(NZ):
        at = slice(hop * wide, (hop + 1) * wide)
        normed = (stream[:, at] * scale * gain[:, at]).astype(BF16)
        sent[:, at] = dot(spots, normed).astype(BF16)


def place_rows(place, blocks, gain, plane):
    rows = blocks[0].shape[0] // (NZ + 1)
    tokens = NZ * rows
    width = NZ * blocks[0].shape[1]
    lanes = plane * NZ * CAP
    return pl.pallas_call(
        place_kernel,
        out_shape=(
            jax.ShapeDtypeStruct((lanes, width), BF16),
            jax.ShapeDtypeStruct((rows, width), F32),
            jax.ShapeDtypeStruct((tokens, lanes), BF16),
            jax.ShapeDtypeStruct((tokens, lanes), BF16),
        ),
        in_specs=[SMEM] + [VMEM] * (NZ + 1),
        out_specs=(VMEM,) * 4,
        scratch_shapes=[
            pltpu.VMEM((tokens, width), F32),
            pltpu.VMEM((tokens, LANES), F32),
            pltpu.VMEM((tokens, lanes), F32),
        ],
        compiler_params=params(32),
    )(place, *blocks, gain.reshape(1, width))


def expert_kernel(first, rows, w_gate, w_up, w_down, out, down, arrived):
    copy = pltpu.make_async_copy(w_down, down, arrived)
    copy.start()
    count, width = out.shape
    deep = width // 4
    gate_act = up_act = 0.0
    for i in range(4):
        at = slice(i * deep, (i + 1) * deep)
        piece = rows[first : first + count, at]
        gate_act += dot(piece, w_gate[0, at, :])
        up_act += dot(piece, w_up[0, at, :])
    hidden = (jax.nn.silu(gate_act) * up_act).astype(BF16)
    copy.wait()
    for i in range(4):
        at = slice(i * deep, (i + 1) * deep)
        out[:, at] = dot(hidden, down[0, :, at]).astype(BF16)


def expert_rows(rows, first, count, w_gate, w_up, w_down):
    return pl.pallas_call(
        functools.partial(expert_kernel, first),
        out_shape=jax.ShapeDtypeStruct((count, rows.shape[1]), BF16),
        in_specs=[VMEM] * 3 + [pl.BlockSpec(memory_space=pl.ANY)],
        out_specs=VMEM,
        scratch_shapes=[pltpu.VMEM(w_down.shape, BF16), pltpu.SemaphoreType.DMA],
        compiler_params=params(32),
        cost_estimate=pl.CostEstimate(
            flops=6 * count * w_down.shape[1] * w_down.shape[2],
            bytes_accessed=6 * w_down.size + 4 * count * rows.shape[1],
            transcendentals=count * w_down.shape[1],
        ),
    )(rows, w_gate, w_up, w_down)


def add_kernel(first, mine, part, *refs):
    out = refs[-1]
    count = part.shape[0]
    if len(refs) > 1:
        out[:first, :] = refs[0][...]
    total = mine[first : first + count, :].astype(F32) + part[...].astype(F32)
    out[first:, :] = total.astype(BF16)


def add_rows(mine, part, *before):
    first = before[0].shape[0] if before else 0
    return pl.pallas_call(
        functools.partial(add_kernel, first),
        out_shape=jax.ShapeDtypeStruct((first + part.shape[0], mine.shape[1]), BF16),
        in_specs=[VMEM] * (2 + len(before)),
        out_specs=VMEM,
        compiler_params=params(32),
    )(mine, part, *before)


def combine_kernel(high, low, back, own, base, *outs):
    rows, width = own.shape
    wide = width // 4
    for i in range(4):
        at = slice(i * wide, (i + 1) * wide)
        piece = back[:, at]
        mix = dot(high[...], piece) + dot(low[...], piece)
        base[:, at] = own[:, at] + mix[:rows]
        for hop in range(1, NZ):
            outs[hop - 1][:, at] = mix[hop * rows : (hop + 1) * rows].astype(BF16)


def combine(high, low, back, own):
    rows, width = own.shape
    return pl.pallas_call(
        combine_kernel,
        out_shape=(jax.ShapeDtypeStruct((rows, width), F32),)
        + (jax.ShapeDtypeStruct((rows, width), BF16),) * (NZ - 1),
        in_specs=[VMEM] * 4,
        out_specs=(VMEM,) * NZ,
        compiler_params=params(32),
    )(high, low, back, own)


def on_device(context, proj_weight, norm_gain, expert_ids, gate_values, w_gate, w_up, w_down):
    zi, xli, ci = (lax.axis_index(a).astype(jnp.int32) for a in ("z", "xl", "c"))
    place = (4 * zi + 2 * xli + ci).reshape(1)
    n_spread = lax.axis_size(SPREAD)
    n_plane = lax.axis_size(PLANE)

    rhs, held = stage(place, proj_weight, swap(proj_weight, "xl"), context)
    give, keep = project(place, [held] + gather_z(context)[1:], rhs, n_spread)
    partial = join(keep, swap(give, "c"))
    partial = lax.all_to_all(partial, SPREAD, 0, 0, tiled=True)

    part = settle(place, partial, expert_ids, gate_values)
    sent, own, high, low = place_rows(place, gather_z(part), norm_gain, n_plane)
    width = sent.shape[1]
    mine = lax.all_to_all(sent.reshape(n_plane, -1, width), PLANE, 0, 0, tiled=True)
    mine = mine.reshape(-1, width)

    weights = (w_gate, w_up, w_down)
    theirs = swap(mine, "c")
    count = mine.shape[0]
    mine_out = expert_rows(mine, 0, count, *weights)
    theirs, mine_out = lax.optimization_barrier((theirs, mine_out))
    half = count // 2
    top, bottom = (swap(expert_rows(theirs, at, half, *weights), "c") for at in (0, half))
    summed = add_rows(mine_out, bottom, add_rows(mine_out, top)).reshape(n_plane, -1, width)
    back = lax.all_to_all(summed, PLANE, 0, 0, tiled=True).reshape(-1, width)

    total, *blocks = combine(high, low, back, own)
    for hop in (2, 6, 3, 5, 4, 1, 7):
        total += fetch(blocks[hop - 1], -hop).astype(F32)
    return total.astype(BF16)


def solution(mesh):
    fine = Mesh(mesh.devices.reshape(SIZES), FINE)
    both = EXPERT + TENSOR
    return jax.shard_map(
        on_device,
        mesh=fine,
        in_specs=(
            P(EXPERT, TENSOR),
            P(TENSOR, EXPERT),
            P(),
            P(both, None),
            P(both, None),
            P(both, None, None),
            P(both, None, None),
            P(both, None, None),
        ),
        out_specs=P(both, None),
        check_vma=False,
    )
```

```python
import functools

import jax
import jax.numpy as jnp
from jax import lax
from jax.experimental import pallas as pl
from jax.experimental.pallas import tpu as pltpu
from jax.sharding import Mesh
from jax.sharding import PartitionSpec as P

TOPK = 8
CAP = 2
LANES = 128
F32, BF16 = jnp.float32, jnp.bfloat16

FINE = ("zh", "zl", "xl", "xh", "y", "c")
SIZES = (4, 2, 2, 2, 4, 2)
EXPERT = ("zh", "zl", "xl")
TENSOR = ("xh", "y", "c")
SPREAD = ("xh", "y")
PEERS = ("zl", "y", "xh", "xl")
RING = ("zh", "zl")
NZ, NH = 8, 4
MIB = 1 << 20

VMEM = pl.BlockSpec(memory_space=pltpu.VMEM)
SMEM = pl.BlockSpec(memory_space=pltpu.SMEM)


def swap(x, axis):
    return lax.ppermute(x, axis, [(0, 1), (1, 0)])


def fetch(x, hop, axis=RING, size=NZ):
    return lax.ppermute(x, axis, [((i + hop) % size, i) for i in range(size)])


def fetch_pair(x, hop):
    return fetch(x, hop, "zh", NH)


def gather_z(x):
    up2, dn2 = fetch(x, 2), fetch(x, -2)
    up1, dn1 = fetch(x, 1), fetch(x, -1)
    up3, dn3 = fetch(up2, 1), fetch(dn2, -1)
    far = fetch(up2, 2)
    return [x, up1, up2, up3, far, dn3, dn2, dn1]


def params(mib):
    return pltpu.CompilerParams(vmem_limit_bytes=mib * MIB)


def dot(a, b):
    return jnp.dot(a, b, preferred_element_type=F32)


def where_am_i(place):
    return lax.div(place[0], 4), lax.rem(lax.div(place[0], 2), 2), lax.rem(place[0], 2)


def stage_kernel(place, own, other, context, rhs, held):
    _, xl, _ = where_am_i(place)
    cols = own.shape[1]
    rhs[:, pl.ds(pl.multiple_of(xl * cols, LANES), cols)] = own[...]
    rhs[:, pl.ds(pl.multiple_of((1 - xl) * cols, LANES), cols)] = other[...]
    held[...] = context[...]


def stage(place, own, other, context):
    return pl.pallas_call(
        stage_kernel,
        out_shape=(
            jax.ShapeDtypeStruct((own.shape[0], 2 * own.shape[1]), BF16),
            jax.ShapeDtypeStruct(context.shape, BF16),
        ),
        in_specs=[SMEM] + [VMEM] * 3,
        out_specs=(VMEM, VMEM),
        compiler_params=params(16),
    )(place, own, other, context)


def project_kernel(place, *refs):
    blocks, (rhs, give, keep, held) = refs[:NZ], refs[NZ:]
    _, _, core = where_am_i(place)
    lhs = jnp.concatenate([b[...] for b in blocks], axis=0)
    total = dot(lhs, rhs[...])
    spread = give.shape[0]
    rows = give.shape[1] // NZ
    total = total.reshape(NZ, spread, 2, rows, rhs.shape[1])
    for k in range(NZ):
        at = slice(k * rows, (k + 1) * rows)
        first, second = total[k, :, 0], total[k, :, 1]
        keep[:, at, :] = jnp.where(core == 0, first, second)
        held[:, at, :] = jnp.where(core == 0, second, first)
    give[...] = held[...].astype(BF16)


def project(place, blocks, rhs, spread):
    rows = blocks[0].shape[0] // (2 * spread)
    shape = (spread, NZ * rows, rhs.shape[1])
    return pl.pallas_call(
        project_kernel,
        out_shape=(jax.ShapeDtypeStruct(shape, BF16), jax.ShapeDtypeStruct(shape, F32)),
        in_specs=[SMEM] + [VMEM] * (NZ + 1),
        out_specs=(VMEM, VMEM),
        scratch_shapes=[pltpu.VMEM(shape, F32)],
        compiler_params=params(32),
    )(place, *blocks, rhs)


def join_kernel(keep, got, out):
    out[...] = (keep[...] + got[...].astype(F32)).astype(BF16)


def join(keep, got):
    return pl.pallas_call(
        join_kernel,
        out_shape=jax.ShapeDtypeStruct(keep.shape, BF16),
        in_specs=[VMEM] * 2,
        out_specs=VMEM,
        compiler_params=params(16),
    )(keep, got)


def settle_kernel(place, parts, mine, give, held):
    z, _, _ = where_am_i(place)
    rows = parts.shape[1] // NZ
    total = parts[0].astype(F32)
    for i in range(1, parts.shape[0]):
        total += parts[i].astype(F32)
    for k in range(NZ):
        at = pl.multiple_of(lax.rem(z + k, NZ) * rows, rows)
        held[pl.ds(at, rows), :] = total[k * rows : (k + 1) * rows]
    for out, parity in ((mine, lax.rem(z, 2)), (give, 1 - lax.rem(z, 2))):
        out[...] = jnp.concatenate(
            [held[pl.ds(pl.multiple_of((2 * i + parity) * rows, rows), rows), :] for i in range(NH)],
            axis=0,
        ).astype(BF16)


def settle(place, parts):
    shape = (parts.shape[1] // 2, parts.shape[2])
    return pl.pallas_call(
        settle_kernel,
        out_shape=(jax.ShapeDtypeStruct(shape, BF16),) * 2,
        in_specs=[SMEM, VMEM],
        out_specs=(VMEM, VMEM),
        scratch_shapes=[pltpu.VMEM(parts.shape[1:], F32)],
        compiler_params=params(16),
    )(place, parts)


def pack_kernel(place, mine, got, ids, gates, out, held):
    z, _, _ = where_am_i(place)
    tokens, cols = mine.shape
    rows = ids.shape[0]
    parity = lax.rem(z, 2)
    held[:tokens, pl.ds(pl.multiple_of(parity * cols, LANES), cols)] = mine[...].astype(F32)
    held[:tokens, pl.ds(pl.multiple_of((1 - parity) * cols, LANES), cols)] = got[...].astype(F32)
    named = ids[...].astype(F32)
    high = gates[...].astype(BF16).astype(F32)
    low = gates[...] - high
    lane = lax.broadcasted_iota(jnp.int32, (rows, held.shape[1]), 1)
    note = jnp.zeros((rows, held.shape[1]), F32)
    for i, part in enumerate((named, high, low)):
        for k in range(TOPK):
            note = jnp.where(lane == i * TOPK + k, part[:, k : k + 1], note)
    held[tokens:, :] = note
    out[...] = held[...].astype(BF16)


def pack(place, mine, got, ids, gates):
    shape = (mine.shape[0] + ids.shape[0], 2 * mine.shape[1])
    return pl.pallas_call(
        pack_kernel,
        out_shape=jax.ShapeDtypeStruct(shape, BF16),
        in_specs=[SMEM] + [VMEM] * 4,
        out_specs=VMEM,
        scratch_shapes=[pltpu.VMEM(shape, F32)],
        compiler_params=params(16),
    )(place, mine, got, ids, gates)


def place_kernel(place, *refs):
    blocks, (gain, sent, own, high, low, stream, notes, mass) = refs[:NH], refs[NH:]
    z, _, _ = where_am_i(place)
    pair = lax.div(z, 2)
    tokens, width = stream.shape
    rows, wide = tokens // NH, width // NH
    lanes = sent.shape[0]
    for hop in range(NH):
        there = lax.rem(pair + hop, NH)
        at = pl.multiple_of(there * wide, LANES)
        block = blocks[hop][...].astype(F32)
        stream[:, pl.ds(at, wide)] = block[:tokens]
        notes[pl.ds(pl.multiple_of(there * rows, rows), rows), :] = block[tokens:, :LANES]
    own[...] = stream[pl.ds(pl.multiple_of(pair * rows, rows), rows), :]

    slots = NH * CAP
    lane = lax.broadcasted_iota(jnp.int32, (tokens, lanes), 1)
    token = lax.broadcasted_iota(jnp.int32, (tokens, lanes), 0)
    peer = lane // slots
    xl, xh, y, zl = peer % 2, (peer // 2) % 2, (peer // 4) % 4, peer // 16
    label = (((pair * 2 + zl) * 2 + xl) * 4 + xh * 2 + y // 2).astype(F32)
    listed = notes[...]
    match = jnp.zeros((tokens, lanes), F32)
    gate = jnp.zeros((tokens, lanes), F32)
    for k in range(TOPK):
        hit = listed[:, k : k + 1] == label
        value = listed[:, TOPK + k : TOPK + k + 1] + listed[:, 2 * TOPK + k : 2 * TOPK + k + 1]
        match += jnp.where(hit, 1.0, 0.0)
        gate += jnp.where(hit, value, 0.0)
    before = lax.broadcasted_iota(jnp.int32, (tokens, tokens), 1)
    after = lax.broadcasted_iota(jnp.int32, (tokens, tokens), 0)
    earlier = (before // rows == after // rows) & (before < after)
    rank = dot(jnp.where(earlier, 1.0, 0.0).astype(BF16), match.astype(BF16))
    slot = (token // rows) * CAP + rank.astype(jnp.int32)
    placed = (match > 0.5) & (slot == lane % slots) & (rank < CAP - 0.5)
    mass[...] = jnp.where(placed, gate, 0.0)
    spots = jnp.transpose(jnp.where(placed, 1.0, 0.0)).astype(BF16)

    weight = jnp.concatenate(
        [
            mass[pl.ds(pl.multiple_of(lax.rem(pair + hop, NH) * rows, rows), rows), :]
            for hop in range(NH)
        ],
        axis=0,
    )
    top = weight.astype(BF16)
    high[...] = top
    low[...] = (weight - top.astype(F32)).astype(BF16)

    square = jnp.zeros((tokens, 1), F32)
    for i in range(NH):
        part = stream[:, i * wide : (i + 1) * wide]
        square += jnp.sum(part * part, axis=-1, keepdims=True)
    scale = lax.rsqrt(square / width + 1e-06)
    for i in range(NH):
        at = slice(i * wide, (i + 1) * wide)
        normed = (stream[:, at] * scale * gain[:, at]).astype(BF16)
        sent[:, at] = dot(spots, normed).astype(BF16)


def place_rows(place, blocks, gain, peers):
    rows = blocks[0].shape[0] // (NH + 1)
    tokens = NH * rows
    width = NH * blocks[0].shape[1]
    lanes = peers * NH * CAP
    return pl.pallas_call(
        place_kernel,
        out_shape=(
            jax.ShapeDtypeStruct((lanes, width), BF16),
            jax.ShapeDtypeStruct((rows, width), F32),
            jax.ShapeDtypeStruct((tokens, lanes), BF16),
            jax.ShapeDtypeStruct((tokens, lanes), BF16),
        ),
        in_specs=[SMEM] + [VMEM] * (NH + 1),
        out_specs=(VMEM,) * 4,
        scratch_shapes=[
            pltpu.VMEM((tokens, width), F32),
            pltpu.VMEM((tokens, LANES), F32),
            pltpu.VMEM((tokens, lanes), F32),
        ],
        compiler_params=params(32),
    )(place, *blocks, gain.reshape(1, width))


def expert_kernel(first, rows, w_gate, w_up, w_down, out, down, arrived):
    copy = pltpu.make_async_copy(w_down, down, arrived)
    copy.start()
    count, width = out.shape
    deep = width // 4
    gate_act = up_act = 0.0
    for i in range(4):
        at = slice(i * deep, (i + 1) * deep)
        piece = rows[first : first + count, at]
        gate_act += dot(piece, w_gate[0, at, :])
        up_act += dot(piece, w_up[0, at, :])
    hidden = (jax.nn.silu(gate_act) * up_act).astype(BF16)
    copy.wait()
    for i in range(4):
        at = slice(i * deep, (i + 1) * deep)
        out[:, at] = dot(hidden, down[0, :, at]).astype(BF16)


def expert_rows(rows, first, count, w_gate, w_up, w_down):
    return pl.pallas_call(
        functools.partial(expert_kernel, first),
        out_shape=jax.ShapeDtypeStruct((count, rows.shape[1]), BF16),
        in_specs=[VMEM] * 3 + [pl.BlockSpec(memory_space=pl.ANY)],
        out_specs=VMEM,
        scratch_shapes=[pltpu.VMEM(w_down.shape, BF16), pltpu.SemaphoreType.DMA],
        compiler_params=params(32),
        cost_estimate=pl.CostEstimate(
            flops=6 * count * w_down.shape[1] * w_down.shape[2],
            bytes_accessed=6 * w_down.size + 4 * count * rows.shape[1],
            transcendentals=count * w_down.shape[1],
        ),
    )(rows, w_gate, w_up, w_down)


def add_kernel(first, mine, part, *refs):
    out = refs[-1]
    count = part.shape[0]
    if len(refs) > 1:
        out[:first, :] = refs[0][...]
    total = mine[first : first + count, :].astype(F32) + part[...].astype(F32)
    out[first:, :] = total.astype(BF16)


def add_rows(mine, part, *before):
    first = before[0].shape[0] if before else 0
    return pl.pallas_call(
        functools.partial(add_kernel, first),
        out_shape=jax.ShapeDtypeStruct((first + part.shape[0], mine.shape[1]), BF16),
        in_specs=[VMEM] * (2 + len(before)),
        out_specs=VMEM,
        compiler_params=params(32),
    )(mine, part, *before)


def combine_kernel(high, low, back, own, base, *outs):
    rows, width = own.shape
    wide = width // 4
    for i in range(4):
        at = slice(i * wide, (i + 1) * wide)
        piece = back[:, at]
        mix = dot(high[...], piece) + dot(low[...], piece)
        base[:, at] = own[:, at] + mix[:rows]
        for hop in range(1, NH):
            outs[hop - 1][:, at] = mix[hop * rows : (hop + 1) * rows].astype(BF16)


def combine(high, low, back, own):
    rows, width = own.shape
    return pl.pallas_call(
        combine_kernel,
        out_shape=(jax.ShapeDtypeStruct((rows, width), F32),)
        + (jax.ShapeDtypeStruct((rows, width), BF16),) * (NH - 1),
        in_specs=[VMEM] * 4,
        out_specs=(VMEM,) * NH,
        compiler_params=params(32),
    )(high, low, back, own)


def on_device(context, proj_weight, norm_gain, expert_ids, gate_values, w_gate, w_up, w_down):
    zi, xli, ci = (lax.axis_index(a).astype(jnp.int32) for a in (RING, "xl", "c"))
    place = (4 * zi + 2 * xli + ci).reshape(1)
    n_spread = lax.axis_size(SPREAD)
    n_peers = lax.axis_size(PEERS)

    rhs, held = stage(place, proj_weight, swap(proj_weight, "xl"), context)
    give, keep = project(place, [held] + gather_z(context)[1:], rhs, n_spread)
    partial = join(keep, swap(give, "c"))
    partial = lax.all_to_all(partial, SPREAD, 0, 0, tiled=True)

    part, give = settle(place, partial)
    part = pack(place, part, swap(give, "zl"), expert_ids, gate_values)
    far, up, dn = fetch_pair(part, 2), fetch_pair(part, 1), fetch_pair(part, -1)
    sent, own, high, low = place_rows(place, [part, up, far, dn], norm_gain, n_peers)
    width = sent.shape[1]
    mine = lax.all_to_all(sent.reshape(n_peers, -1, width), PEERS, 0, 0, tiled=True)
    mine = mine.reshape(-1, width)

    weights = (w_gate, w_up, w_down)
    theirs = swap(mine, "c")
    count = mine.shape[0]
    mine_out = expert_rows(mine, 0, count, *weights)
    theirs, mine_out = lax.optimization_barrier((theirs, mine_out))
    half = count // 2
    top, bottom = (swap(expert_rows(theirs, at, half, *weights), "c") for at in (0, half))
    summed = add_rows(mine_out, bottom, add_rows(mine_out, top)).reshape(n_peers, -1, width)
    back = lax.all_to_all(summed, PEERS, 0, 0, tiled=True).reshape(-1, width)

    total, *blocks = combine(high, low, back, own)
    for hop in (2, 1, 3):
        total += fetch_pair(blocks[hop - 1], -hop).astype(F32)
    return total.astype(BF16)


def solution(mesh):
    fine = Mesh(mesh.devices.reshape(SIZES), FINE)
    both = EXPERT + TENSOR
    return jax.shard_map(
        on_device,
        mesh=fine,
        in_specs=(
            P(EXPERT, TENSOR),
            P(TENSOR, EXPERT),
            P(),
            P(both, None),
            P(both, None),
            P(both, None, None),
            P(both, None, None),
            P(both, None, None),
        ),
        out_specs=P(both, None),
        check_vma=False,
    )
```

```python
import functools

import jax
import jax.numpy as jnp
from jax import lax
from jax.experimental import pallas as pl
from jax.experimental.pallas import tpu as pltpu
from jax.sharding import Mesh
from jax.sharding import PartitionSpec as P

TOPK = 8
CAP = 2
ROWS = 8
LANES = 128
F32, BF16 = jnp.float32, jnp.bfloat16

FINE = ("zh", "zl", "xl", "xh", "y", "c")
SIZES = (4, 2, 2, 2, 4, 2)
EXPERT = ("zh", "zl", "xl")
TENSOR = ("xh", "y", "c")
SPREAD = ("xh", "y")
PLANE = ("y", "xh", "xl")
PEERS = ("y", "xh", "xl", "zl")
RING = ("zh", "zl")
NZ, NH = 8, 4
MIB = 1 << 20

VMEM = pl.BlockSpec(memory_space=pltpu.VMEM)
SMEM = pl.BlockSpec(memory_space=pltpu.SMEM)


def swap(x, axis):
    return lax.ppermute(x, axis, [(0, 1), (1, 0)])


def fetch(x, hop, axis=RING, size=NZ):
    return lax.ppermute(x, axis, [((i + hop) % size, i) for i in range(size)])


def fetch_pair(x, hop):
    return fetch(x, hop, "zh", NH)


def gather_z(x):
    up2, dn2 = fetch(x, 2), fetch(x, -2)
    up1, dn1 = fetch(x, 1), fetch(x, -1)
    up3, dn3 = fetch(up2, 1), fetch(dn2, -1)
    far = fetch(up2, 2)
    return [x, up1, up2, up3, far, dn3, dn2, dn1]


def params(mib):
    return pltpu.CompilerParams(vmem_limit_bytes=mib * MIB)


def dot(a, b):
    return jnp.dot(a, b, preferred_element_type=F32)


def where_am_i(place):
    return lax.div(place[0], 4), lax.rem(lax.div(place[0], 2), 2), lax.rem(place[0], 2)


def stage_kernel(place, own, other, context, rhs, held):
    _, xl, _ = where_am_i(place)
    cols = own.shape[1]
    rhs[:, pl.ds(pl.multiple_of(xl * cols, LANES), cols)] = own[...]
    rhs[:, pl.ds(pl.multiple_of((1 - xl) * cols, LANES), cols)] = other[...]
    held[...] = context[...]


def stage(place, own, other, context):
    return pl.pallas_call(
        stage_kernel,
        out_shape=(
            jax.ShapeDtypeStruct((own.shape[0], 2 * own.shape[1]), BF16),
            jax.ShapeDtypeStruct(context.shape, BF16),
        ),
        in_specs=[SMEM] + [VMEM] * 3,
        out_specs=(VMEM, VMEM),
        compiler_params=params(16),
    )(place, own, other, context)


def project_kernel(place, *refs):
    blocks, (rhs, give, keep, held) = refs[:NZ], refs[NZ:]
    _, _, core = where_am_i(place)
    lhs = jnp.concatenate([b[...] for b in blocks], axis=0)
    total = dot(lhs, rhs[...])
    spread = give.shape[0]
    rows = give.shape[1] // NZ
    total = total.reshape(NZ, spread, 2, rows, rhs.shape[1])
    for k in range(NZ):
        at = slice(k * rows, (k + 1) * rows)
        first, second = total[k, :, 0], total[k, :, 1]
        keep[:, at, :] = jnp.where(core == 0, first, second)
        held[:, at, :] = jnp.where(core == 0, second, first)
    give[...] = held[...].astype(BF16)


def project(place, blocks, rhs, spread):
    rows = blocks[0].shape[0] // (2 * spread)
    shape = (spread, NZ * rows, rhs.shape[1])
    return pl.pallas_call(
        project_kernel,
        out_shape=(jax.ShapeDtypeStruct(shape, BF16), jax.ShapeDtypeStruct(shape, F32)),
        in_specs=[SMEM] + [VMEM] * (NZ + 1),
        out_specs=(VMEM, VMEM),
        scratch_shapes=[pltpu.VMEM(shape, F32)],
        compiler_params=params(32),
    )(place, *blocks, rhs)


def join_kernel(keep, got, out):
    out[...] = (keep[...] + got[...].astype(F32)).astype(BF16)


def join(keep, got):
    return pl.pallas_call(
        join_kernel,
        out_shape=jax.ShapeDtypeStruct(keep.shape, BF16),
        in_specs=[VMEM] * 2,
        out_specs=VMEM,
        compiler_params=params(16),
    )(keep, got)


def settle_kernel(place, parts, ids, gates, out, held):
    z, _, _ = where_am_i(place)
    tokens = parts.shape[1]
    rows = tokens // NZ
    total = parts[0].astype(F32)
    for i in range(1, parts.shape[0]):
        total += parts[i].astype(F32)
    for k in range(NZ):
        at = pl.multiple_of(lax.rem(z + k, NZ) * rows, rows)
        held[pl.ds(at, rows), :] = total[k * rows : (k + 1) * rows]
    named = ids[...].astype(F32)
    high = gates[...].astype(BF16).astype(F32)
    low = gates[...] - high
    lane = lax.broadcasted_iota(jnp.int32, (rows, held.shape[1]), 1)
    note = jnp.zeros((rows, held.shape[1]), F32)
    for i, part in enumerate((named, high, low)):
        for k in range(TOPK):
            note = jnp.where(lane == i * TOPK + k, part[:, k : k + 1], note)
    held[tokens:, :] = note
    out[...] = held[...].astype(BF16)


def settle(place, parts, ids, gates):
    shape = (parts.shape[1] + ids.shape[0], parts.shape[2])
    return pl.pallas_call(
        settle_kernel,
        out_shape=jax.ShapeDtypeStruct(shape, BF16),
        in_specs=[SMEM, VMEM, VMEM, VMEM],
        out_specs=VMEM,
        scratch_shapes=[pltpu.VMEM(shape, F32)],
        compiler_params=params(16),
    )(place, parts, ids, gates)


def routed(listed, label, spot):
    tokens, rows = listed.shape[0], ROWS
    match = jnp.zeros(label.shape, F32)
    gate = jnp.zeros(label.shape, F32)
    for k in range(TOPK):
        hit = listed[:, k : k + 1] == label.astype(F32)
        value = listed[:, TOPK + k : TOPK + k + 1] + listed[:, 2 * TOPK + k : 2 * TOPK + k + 1]
        match += jnp.where(hit, 1.0, 0.0)
        gate += jnp.where(hit, value, 0.0)
    before = lax.broadcasted_iota(jnp.int32, (tokens, tokens), 1)
    after = lax.broadcasted_iota(jnp.int32, (tokens, tokens), 0)
    earlier = (before // rows == after // rows) & (before < after)
    rank = dot(jnp.where(earlier, 1.0, 0.0).astype(BF16), match.astype(BF16))
    placed = (match > 0.5) & (rank.astype(jnp.int32) == spot)
    return placed, gate


def place_kernel(place, *refs):
    blocks, (gain, sent, own, high, low, stream, notes) = refs[:NZ], refs[NZ:]
    z, _, _ = where_am_i(place)
    pair, parity = lax.div(z, 2), lax.rem(z, 2)
    tokens, width = stream.shape
    rows, wide = ROWS, width // NZ
    lanes = sent.shape[0]
    for hop in range(NZ):
        there = lax.rem(z + hop, NZ)
        at = pl.multiple_of(there * wide, LANES)
        block = blocks[hop][...].astype(F32)
        stream[:, pl.ds(at, wide)] = block[:tokens]
        notes[pl.ds(pl.multiple_of(there * rows, rows), rows), :] = block[tokens:, :LANES]
    own[...] = stream[pl.ds(pl.multiple_of(z * rows, rows), rows), :]

    lane = lax.broadcasted_iota(jnp.int32, (tokens, lanes), 1)
    from_z = lax.broadcasted_iota(jnp.int32, (tokens, lanes), 0) // rows
    slot, device = lane % (NZ * CAP), lane // (NZ * CAP)
    label = (z * 2 + device % 2) * 4 + (device // 2) % 2 * 2 + device // 8
    spot = slot - (from_z % 2) * (NH * CAP) - (from_z // 2) * CAP
    placed, _ = routed(notes[...], label, spot)
    spots = jnp.transpose(jnp.where(placed, 1.0, 0.0)).astype(BF16)

    half = tokens // 2
    near = [lax.rem(pair + hop, NH) for hop in range(NH)]
    listed = jnp.concatenate(
        [notes[pl.ds(pl.multiple_of((2 * n + parity) * rows, rows), rows), :] for n in near],
        axis=0,
    )
    lane = lax.broadcasted_iota(jnp.int32, (half, lanes), 1)
    hop = lax.broadcasted_iota(jnp.int32, (half, lanes), 0) // rows
    slot, peer = lane % (NH * CAP), lane // (NH * CAP)
    label = ((pair * 2 + peer % 2) * 2 + (peer // 2) % 2) * 4 + (peer // 4) % 2 * 2 + peer // 16
    placed, gate = routed(listed, label, slot - ((pair + hop) % NH) * CAP)
    weight = jnp.where(placed, gate, 0.0)
    top = weight.astype(BF16)
    high[...] = top
    low[...] = (weight - top.astype(F32)).astype(BF16)

    square = jnp.zeros((tokens, 1), F32)
    for i in range(NZ):
        part = stream[:, i * wide : (i + 1) * wide]
        square += jnp.sum(part * part, axis=-1, keepdims=True)
    scale = lax.rsqrt(square / width + 1e-06)
    for i in range(NZ):
        at = slice(i * wide, (i + 1) * wide)
        normed = (stream[:, at] * scale * gain[:, at]).astype(BF16)
        sent[:, at] = dot(spots, normed).astype(BF16)


def place_rows(place, blocks, gain, plane):
    tokens = NZ * ROWS
    width = NZ * blocks[0].shape[1]
    lanes = plane * NZ * CAP
    return pl.pallas_call(
        place_kernel,
        out_shape=(
            jax.ShapeDtypeStruct((lanes, width), BF16),
            jax.ShapeDtypeStruct((ROWS, width), F32),
            jax.ShapeDtypeStruct((tokens // 2, lanes), BF16),
            jax.ShapeDtypeStruct((tokens // 2, lanes), BF16),
        ),
        in_specs=[SMEM] + [VMEM] * (NZ + 1),
        out_specs=(VMEM,) * 4,
        scratch_shapes=[
            pltpu.VMEM((tokens, width), F32),
            pltpu.VMEM((tokens, LANES), F32),
        ],
        compiler_params=params(32),
    )(place, *blocks, gain.reshape(1, width))


def expert_kernel(first, rows, w_gate, w_up, w_down, out, down, arrived):
    copy = pltpu.make_async_copy(w_down, down, arrived)
    copy.start()
    count, width = out.shape
    deep = width // 4
    gate_act = up_act = 0.0
    for i in range(4):
        at = slice(i * deep, (i + 1) * deep)
        piece = rows[first : first + count, at]
        gate_act += dot(piece, w_gate[0, at, :])
        up_act += dot(piece, w_up[0, at, :])
    hidden = (jax.nn.silu(gate_act) * up_act).astype(BF16)
    copy.wait()
    for i in range(4):
        at = slice(i * deep, (i + 1) * deep)
        out[:, at] = dot(hidden, down[0, :, at]).astype(BF16)


def expert_rows(rows, first, count, w_gate, w_up, w_down):
    return pl.pallas_call(
        functools.partial(expert_kernel, first),
        out_shape=jax.ShapeDtypeStruct((count, rows.shape[1]), BF16),
        in_specs=[VMEM] * 3 + [pl.BlockSpec(memory_space=pl.ANY)],
        out_specs=VMEM,
        scratch_shapes=[pltpu.VMEM(w_down.shape, BF16), pltpu.SemaphoreType.DMA],
        compiler_params=params(32),
        cost_estimate=pl.CostEstimate(
            flops=6 * count * w_down.shape[1] * w_down.shape[2],
            bytes_accessed=6 * w_down.size + 4 * count * rows.shape[1],
            transcendentals=count * w_down.shape[1],
        ),
    )(rows, w_gate, w_up, w_down)


def add_kernel(first, mine, part, *refs):
    out = refs[-1]
    count = part.shape[0]
    if len(refs) > 1:
        out[:first, :] = refs[0][...]
    total = mine[first : first + count, :].astype(F32) + part[...].astype(F32)
    out[first:, :] = total.astype(BF16)


def add_rows(mine, part, *before):
    first = before[0].shape[0] if before else 0
    return pl.pallas_call(
        functools.partial(add_kernel, first),
        out_shape=jax.ShapeDtypeStruct((first + part.shape[0], mine.shape[1]), BF16),
        in_specs=[VMEM] * (2 + len(before)),
        out_specs=VMEM,
        compiler_params=params(32),
    )(mine, part, *before)


def combine_kernel(high, low, back, own, base, *outs):
    rows, width = own.shape
    wide = width // 4
    for i in range(4):
        at = slice(i * wide, (i + 1) * wide)
        piece = back[:, at]
        mix = dot(high[...], piece) + dot(low[...], piece)
        base[:, at] = own[:, at] + mix[:rows]
        for hop in range(1, NH):
            outs[hop - 1][:, at] = mix[hop * rows : (hop + 1) * rows].astype(BF16)


def combine(high, low, back, own):
    rows, width = own.shape
    return pl.pallas_call(
        combine_kernel,
        out_shape=(jax.ShapeDtypeStruct((rows, width), F32),)
        + (jax.ShapeDtypeStruct((rows, width), BF16),) * (NH - 1),
        in_specs=[VMEM] * 4,
        out_specs=(VMEM,) * NH,
        compiler_params=params(32),
    )(high, low, back, own)


def on_device(context, proj_weight, norm_gain, expert_ids, gate_values, w_gate, w_up, w_down):
    zi, xli, ci = (lax.axis_index(a).astype(jnp.int32) for a in (RING, "xl", "c"))
    place = (4 * zi + 2 * xli + ci).reshape(1)
    n_spread = lax.axis_size(SPREAD)
    n_plane, n_peers = lax.axis_size(PLANE), lax.axis_size(PEERS)

    rhs, held = stage(place, proj_weight, swap(proj_weight, "xl"), context)
    give, keep = project(place, [held] + gather_z(context)[1:], rhs, n_spread)
    partial = join(keep, swap(give, "c"))
    partial = lax.all_to_all(partial, SPREAD, 0, 0, tiled=True)

    part = settle(place, partial, expert_ids, gate_values)
    sent, own, high, low = place_rows(place, gather_z(part), norm_gain, n_plane)
    width = sent.shape[1]
    mine = lax.all_to_all(sent.reshape(n_plane, -1, width), PLANE, 0, 0, tiled=True)
    mine = mine.reshape(-1, width)

    weights = (w_gate, w_up, w_down)
    theirs = swap(mine, "c")
    count = mine.shape[0]
    mine_out = expert_rows(mine, 0, count, *weights)
    theirs, mine_out = lax.optimization_barrier((theirs, mine_out))
    half = count // 2
    top, bottom = (swap(expert_rows(theirs, at, half, *weights), "c") for at in (0, half))
    summed = add_rows(mine_out, bottom, add_rows(mine_out, top)).reshape(n_peers, -1, width)
    back = lax.all_to_all(summed, PEERS, 0, 0, tiled=True).reshape(-1, width)

    total, *blocks = combine(high, low, back, own)
    for hop in (2, 1, 3):
        total += fetch_pair(blocks[hop - 1], -hop).astype(F32)
    return total.astype(BF16)


def solution(mesh):
    fine = Mesh(mesh.devices.reshape(SIZES), FINE)
    both = EXPERT + TENSOR
    return jax.shard_map(
        on_device,
        mesh=fine,
        in_specs=(
            P(EXPERT, TENSOR),
            P(TENSOR, EXPERT),
            P(),
            P(both, None),
            P(both, None),
            P(both, None, None),
            P(both, None, None),
            P(both, None, None),
        ),
        out_specs=P(both, None),
        check_vma=False,
    )
```

```python
import functools

import jax
import jax.numpy as jnp
from jax import lax
from jax.experimental import pallas as pl
from jax.experimental.pallas import tpu as pltpu
from jax.sharding import Mesh
from jax.sharding import PartitionSpec as P

TOPK = 8
CAP = 2
ROWS = 8
LANES = 128
F32, BF16 = jnp.float32, jnp.bfloat16

FINE = ("zh", "zl", "xl", "xh", "y", "c")
SIZES = (4, 2, 2, 2, 4, 2)
EXPERT = ("zh", "zl", "xl")
TENSOR = ("xh", "y", "c")
SPREAD = ("xh", "y")
PLANE = ("y", "xl", "xh")
PEERS = ("y", "xl", "xh", "zl")
RING = ("zh", "zl")
NZ, NH = 8, 4
MIB = 1 << 20

VMEM = pl.BlockSpec(memory_space=pltpu.VMEM)
SMEM = pl.BlockSpec(memory_space=pltpu.SMEM)


def swap(x, axis):
    return lax.ppermute(x, axis, [(0, 1), (1, 0)])


def fetch(x, hop, axis=RING, size=NZ):
    return lax.ppermute(x, axis, [((i + hop) % size, i) for i in range(size)])


def fetch_pair(x, hop):
    return fetch(x, hop, "zh", NH)


def gather_z(x):
    up2, dn2 = fetch(x, 2), fetch(x, -2)
    up1, dn1 = fetch(x, 1), fetch(x, -1)
    up3, dn3 = fetch(up2, 1), fetch(dn2, -1)
    far = fetch(up2, 2)
    return [x, up1, up2, up3, far, dn3, dn2, dn1]


def params(mib):
    return pltpu.CompilerParams(vmem_limit_bytes=mib * MIB)


def dot(a, b):
    return jnp.dot(a, b, preferred_element_type=F32)


def where_am_i(place):
    return lax.div(place[0], 4), lax.rem(lax.div(place[0], 2), 2), lax.rem(place[0], 2)


def stage_kernel(place, own, other, context, rhs, held):
    _, xl, _ = where_am_i(place)
    cols = own.shape[1]
    rhs[:, pl.ds(pl.multiple_of(xl * cols, LANES), cols)] = own[...]
    rhs[:, pl.ds(pl.multiple_of((1 - xl) * cols, LANES), cols)] = other[...]
    held[...] = context[...]


def stage(place, own, other, context):
    return pl.pallas_call(
        stage_kernel,
        out_shape=(
            jax.ShapeDtypeStruct((own.shape[0], 2 * own.shape[1]), BF16),
            jax.ShapeDtypeStruct(context.shape, BF16),
        ),
        in_specs=[SMEM] + [VMEM] * 3,
        out_specs=(VMEM, VMEM),
        compiler_params=params(16),
    )(place, own, other, context)


def project_kernel(place, *refs):
    blocks, (rhs, give, keep, held) = refs[:NZ], refs[NZ:]
    _, _, core = where_am_i(place)
    lhs = jnp.concatenate([b[...] for b in blocks], axis=0)
    total = dot(lhs, rhs[...])
    spread = give.shape[0]
    rows = give.shape[1] // NZ
    total = total.reshape(NZ, spread, 2, rows, rhs.shape[1])
    for k in range(NZ):
        at = slice(k * rows, (k + 1) * rows)
        first, second = total[k, :, 0], total[k, :, 1]
        keep[:, at, :] = jnp.where(core == 0, first, second)
        held[:, at, :] = jnp.where(core == 0, second, first)
    give[...] = held[...].astype(BF16)


def project(place, blocks, rhs, spread):
    rows = blocks[0].shape[0] // (2 * spread)
    shape = (spread, NZ * rows, rhs.shape[1])
    return pl.pallas_call(
        project_kernel,
        out_shape=(jax.ShapeDtypeStruct(shape, BF16), jax.ShapeDtypeStruct(shape, F32)),
        in_specs=[SMEM] + [VMEM] * (NZ + 1),
        out_specs=(VMEM, VMEM),
        scratch_shapes=[pltpu.VMEM(shape, F32)],
        compiler_params=params(32),
    )(place, *blocks, rhs)


def join_kernel(keep, got, out):
    out[...] = (keep[...] + got[...].astype(F32)).astype(BF16)


def join(keep, got):
    return pl.pallas_call(
        join_kernel,
        out_shape=jax.ShapeDtypeStruct(keep.shape, BF16),
        in_specs=[VMEM] * 2,
        out_specs=VMEM,
        compiler_params=params(16),
    )(keep, got)


def settle_kernel(place, parts, ids, gates, out, held):
    z, _, _ = where_am_i(place)
    tokens = parts.shape[1]
    rows = tokens // NZ
    total = parts[0].astype(F32)
    for i in range(1, parts.shape[0]):
        total += parts[i].astype(F32)
    for k in range(NZ):
        at = pl.multiple_of(lax.rem(z + k, NZ) * rows, rows)
        held[pl.ds(at, rows), :] = total[k * rows : (k + 1) * rows]
    named = ids[...].astype(F32)
    high = gates[...].astype(BF16).astype(F32)
    low = gates[...] - high
    lane = lax.broadcasted_iota(jnp.int32, (rows, held.shape[1]), 1)
    note = jnp.zeros((rows, held.shape[1]), F32)
    for i, part in enumerate((named, high, low)):
        for k in range(TOPK):
            note = jnp.where(lane == i * TOPK + k, part[:, k : k + 1], note)
    held[tokens:, :] = note
    out[...] = held[...].astype(BF16)


def settle(place, parts, ids, gates):
    shape = (parts.shape[1] + ids.shape[0], parts.shape[2])
    return pl.pallas_call(
        settle_kernel,
        out_shape=jax.ShapeDtypeStruct(shape, BF16),
        in_specs=[SMEM, VMEM, VMEM, VMEM],
        out_specs=VMEM,
        scratch_shapes=[pltpu.VMEM(shape, F32)],
        compiler_params=params(16),
    )(place, parts, ids, gates)


def coords(index, axes):
    found = {}
    for axis in reversed(axes):
        size = SIZES[FINE.index(axis)]
        found[axis] = index % size
        index = index // size
    return found


def label_of(z, at):
    return (z * 2 + at["xl"]) * 4 + at["xh"] * 2 + at["y"] // 2


def routed(listed, label, spot):
    tokens, rows = listed.shape[0], ROWS
    match = jnp.zeros(label.shape, F32)
    gate = jnp.zeros(label.shape, F32)
    for k in range(TOPK):
        hit = listed[:, k : k + 1] == label.astype(F32)
        value = listed[:, TOPK + k : TOPK + k + 1] + listed[:, 2 * TOPK + k : 2 * TOPK + k + 1]
        match += jnp.where(hit, 1.0, 0.0)
        gate += jnp.where(hit, value, 0.0)
    before = lax.broadcasted_iota(jnp.int32, (tokens, tokens), 1)
    after = lax.broadcasted_iota(jnp.int32, (tokens, tokens), 0)
    earlier = (before // rows == after // rows) & (before < after)
    rank = dot(jnp.where(earlier, 1.0, 0.0).astype(BF16), match.astype(BF16))
    placed = (match > 0.5) & (rank.astype(jnp.int32) == spot)
    return placed, gate


def place_kernel(place, *refs):
    blocks, (gain, sent, own, high, low, stream, notes) = refs[:NZ], refs[NZ:]
    z, _, _ = where_am_i(place)
    pair, parity = lax.div(z, 2), lax.rem(z, 2)
    tokens, width = stream.shape
    rows, wide = ROWS, width // NZ
    lanes = sent.shape[0]
    for hop in range(NZ):
        there = lax.rem(z + hop, NZ)
        at = pl.multiple_of(there * wide, LANES)
        block = blocks[hop][...].astype(F32)
        stream[:, pl.ds(at, wide)] = block[:tokens]
        notes[pl.ds(pl.multiple_of(there * rows, rows), rows), :] = block[tokens:, :LANES]
    own[...] = stream[pl.ds(pl.multiple_of(z * rows, rows), rows), :]

    lane = lax.broadcasted_iota(jnp.int32, (tokens, lanes), 1)
    from_z = lax.broadcasted_iota(jnp.int32, (tokens, lanes), 0) // rows
    slot, device = lane % (NZ * CAP), lane // (NZ * CAP)
    label = label_of(z, coords(device, PLANE))
    spot = slot - (from_z % 2) * (NH * CAP) - (from_z // 2) * CAP
    placed, _ = routed(notes[...], label, spot)
    spots = jnp.transpose(jnp.where(placed, 1.0, 0.0)).astype(BF16)

    half = tokens // 2
    near = [lax.rem(pair + hop, NH) for hop in range(NH)]
    listed = jnp.concatenate(
        [notes[pl.ds(pl.multiple_of((2 * n + parity) * rows, rows), rows), :] for n in near],
        axis=0,
    )
    lane = lax.broadcasted_iota(jnp.int32, (half, lanes), 1)
    hop = lax.broadcasted_iota(jnp.int32, (half, lanes), 0) // rows
    slot, peer = lane % (NH * CAP), lane // (NH * CAP)
    at = coords(peer, PEERS)
    label = label_of(pair * 2 + at["zl"], at)
    placed, gate = routed(listed, label, slot - ((pair + hop) % NH) * CAP)
    weight = jnp.where(placed, gate, 0.0)
    top = weight.astype(BF16)
    high[...] = top
    low[...] = (weight - top.astype(F32)).astype(BF16)

    square = jnp.zeros((tokens, 1), F32)
    for i in range(NZ):
        part = stream[:, i * wide : (i + 1) * wide]
        square += jnp.sum(part * part, axis=-1, keepdims=True)
    scale = lax.rsqrt(square / width + 1e-06)
    for i in range(NZ):
        at = slice(i * wide, (i + 1) * wide)
        normed = (stream[:, at] * scale * gain[:, at]).astype(BF16)
        sent[:, at] = dot(spots, normed).astype(BF16)


def place_rows(place, blocks, gain, plane):
    tokens = NZ * ROWS
    width = NZ * blocks[0].shape[1]
    lanes = plane * NZ * CAP
    return pl.pallas_call(
        place_kernel,
        out_shape=(
            jax.ShapeDtypeStruct((lanes, width), BF16),
            jax.ShapeDtypeStruct((ROWS, width), F32),
            jax.ShapeDtypeStruct((tokens // 2, lanes), BF16),
            jax.ShapeDtypeStruct((tokens // 2, lanes), BF16),
        ),
        in_specs=[SMEM] + [VMEM] * (NZ + 1),
        out_specs=(VMEM,) * 4,
        scratch_shapes=[
            pltpu.VMEM((tokens, width), F32),
            pltpu.VMEM((tokens, LANES), F32),
        ],
        compiler_params=params(32),
    )(place, *blocks, gain.reshape(1, width))


def expert_kernel(first, rows, w_gate, w_up, w_down, out, down, arrived):
    copy = pltpu.make_async_copy(w_down, down, arrived)
    copy.start()
    count, width = out.shape
    deep = width // 4
    gate_act = up_act = 0.0
    for i in range(4):
        at = slice(i * deep, (i + 1) * deep)
        piece = rows[first : first + count, at]
        gate_act += dot(piece, w_gate[0, at, :])
        up_act += dot(piece, w_up[0, at, :])
    hidden = (jax.nn.silu(gate_act) * up_act).astype(BF16)
    copy.wait()
    for i in range(4):
        at = slice(i * deep, (i + 1) * deep)
        out[:, at] = dot(hidden, down[0, :, at]).astype(BF16)


def expert_rows(rows, first, count, w_gate, w_up, w_down):
    return pl.pallas_call(
        functools.partial(expert_kernel, first),
        out_shape=jax.ShapeDtypeStruct((count, rows.shape[1]), BF16),
        in_specs=[VMEM] * 3 + [pl.BlockSpec(memory_space=pl.ANY)],
        out_specs=VMEM,
        scratch_shapes=[pltpu.VMEM(w_down.shape, BF16), pltpu.SemaphoreType.DMA],
        compiler_params=params(32),
        cost_estimate=pl.CostEstimate(
            flops=6 * count * w_down.shape[1] * w_down.shape[2],
            bytes_accessed=6 * w_down.size + 4 * count * rows.shape[1],
            transcendentals=count * w_down.shape[1],
        ),
    )(rows, w_gate, w_up, w_down)


def add_kernel(first, mine, part, *refs):
    out = refs[-1]
    count = part.shape[0]
    if len(refs) > 1:
        out[:first, :] = refs[0][...]
    total = mine[first : first + count, :].astype(F32) + part[...].astype(F32)
    out[first:, :] = total.astype(BF16)


def add_rows(mine, part, *before):
    first = before[0].shape[0] if before else 0
    return pl.pallas_call(
        functools.partial(add_kernel, first),
        out_shape=jax.ShapeDtypeStruct((first + part.shape[0], mine.shape[1]), BF16),
        in_specs=[VMEM] * (2 + len(before)),
        out_specs=VMEM,
        compiler_params=params(32),
    )(mine, part, *before)


def combine_kernel(high, low, back, own, base, *outs):
    rows, width = own.shape
    wide = width // 4
    for i in range(4):
        at = slice(i * wide, (i + 1) * wide)
        piece = back[:, at]
        mix = dot(high[...], piece) + dot(low[...], piece)
        base[:, at] = own[:, at] + mix[:rows]
        for hop in range(1, NH):
            outs[hop - 1][:, at] = mix[hop * rows : (hop + 1) * rows].astype(BF16)


def combine(high, low, back, own):
    rows, width = own.shape
    return pl.pallas_call(
        combine_kernel,
        out_shape=(jax.ShapeDtypeStruct((rows, width), F32),)
        + (jax.ShapeDtypeStruct((rows, width), BF16),) * (NH - 1),
        in_specs=[VMEM] * 4,
        out_specs=(VMEM,) * NH,
        compiler_params=params(32),
    )(high, low, back, own)


def on_device(context, proj_weight, norm_gain, expert_ids, gate_values, w_gate, w_up, w_down):
    zi, xli, ci = (lax.axis_index(a).astype(jnp.int32) for a in (RING, "xl", "c"))
    place = (4 * zi + 2 * xli + ci).reshape(1)
    n_spread = lax.axis_size(SPREAD)
    n_plane, n_peers = lax.axis_size(PLANE), lax.axis_size(PEERS)

    rhs, held = stage(place, proj_weight, swap(proj_weight, "xl"), context)
    give, keep = project(place, [held] + gather_z(context)[1:], rhs, n_spread)
    partial = join(keep, swap(give, "c"))
    partial = lax.all_to_all(partial, SPREAD, 0, 0, tiled=True)

    part = settle(place, partial, expert_ids, gate_values)
    sent, own, high, low = place_rows(place, gather_z(part), norm_gain, n_plane)
    width = sent.shape[1]
    mine = lax.all_to_all(sent.reshape(n_plane, -1, width), PLANE, 0, 0, tiled=True)
    mine = mine.reshape(-1, width)

    weights = (w_gate, w_up, w_down)
    theirs = swap(mine, "c")
    count = mine.shape[0]
    mine_out = expert_rows(mine, 0, count, *weights)
    theirs, mine_out = lax.optimization_barrier((theirs, mine_out))
    half = count // 2
    top, bottom = (swap(expert_rows(theirs, at, half, *weights), "c") for at in (0, half))
    summed = add_rows(mine_out, bottom, add_rows(mine_out, top)).reshape(n_peers, -1, width)
    back = lax.all_to_all(summed, PEERS, 0, 0, tiled=True).reshape(-1, width)

    total, *blocks = combine(high, low, back, own)
    for hop in (2, 1, 3):
        total += fetch_pair(blocks[hop - 1], -hop).astype(F32)
    return total.astype(BF16)


def solution(mesh):
    fine = Mesh(mesh.devices.reshape(SIZES), FINE)
    both = EXPERT + TENSOR
    return jax.shard_map(
        on_device,
        mesh=fine,
        in_specs=(
            P(EXPERT, TENSOR),
            P(TENSOR, EXPERT),
            P(),
            P(both, None),
            P(both, None),
            P(both, None, None),
            P(both, None, None),
            P(both, None, None),
        ),
        out_specs=P(both, None),
        check_vma=False,
    )
```

```python
import functools

import jax
import jax.numpy as jnp
from jax import lax
from jax.experimental import pallas as pl
from jax.experimental.pallas import tpu as pltpu
from jax.sharding import Mesh
from jax.sharding import PartitionSpec as P

TOPK = 8
CAP = 2
ROWS = 8
LANES = 128
F32, BF16 = jnp.float32, jnp.bfloat16

FINE = ("zh", "zl", "xl", "xh", "y", "c")
SIZES = (4, 2, 2, 2, 4, 2)
EXPERT = ("zh", "zl", "xl")
TENSOR = ("xh", "y", "c")
SPREAD = ("xh", "y")
PLANE = ("y", "xl", "xh")
PEERS = ("y", "xl", "xh", "zl")
RING = ("zh", "zl")
NZ, NH = 8, 4
MIB = 1 << 20

VMEM = pl.BlockSpec(memory_space=pltpu.VMEM)
SMEM = pl.BlockSpec(memory_space=pltpu.SMEM)


def swap(x, axis):
    return lax.ppermute(x, axis, [(0, 1), (1, 0)])


def fetch(x, hop, axis=RING, size=NZ):
    return lax.ppermute(x, axis, [((i + hop) % size, i) for i in range(size)])


def fetch_pair(x, hop):
    return fetch(x, hop, "zh", NH)


def gather_z(x):
    up2, dn2 = fetch(x, 2), fetch(x, -2)
    up1, dn1 = fetch(x, 1), fetch(x, -1)
    up3, dn3 = fetch(up2, 1), fetch(dn2, -1)
    far = fetch(up2, 2)
    return [x, up1, up2, up3, far, dn3, dn2, dn1]


def params(mib):
    return pltpu.CompilerParams(vmem_limit_bytes=mib * MIB)


def dot(a, b):
    return jnp.dot(a, b, preferred_element_type=F32)


def where_am_i(place):
    return lax.div(place[0], 4), lax.rem(lax.div(place[0], 2), 2), lax.rem(place[0], 2)


def stage_kernel(place, own, other, context, rhs, held):
    _, xl, _ = where_am_i(place)
    cols = own.shape[1]
    rhs[:, pl.ds(pl.multiple_of(xl * cols, LANES), cols)] = own[...]
    rhs[:, pl.ds(pl.multiple_of((1 - xl) * cols, LANES), cols)] = other[...]
    held[...] = context[...]


def stage(place, own, other, context):
    return pl.pallas_call(
        stage_kernel,
        out_shape=(
            jax.ShapeDtypeStruct((own.shape[0], 2 * own.shape[1]), BF16),
            jax.ShapeDtypeStruct(context.shape, BF16),
        ),
        in_specs=[SMEM] + [VMEM] * 3,
        out_specs=(VMEM, VMEM),
        compiler_params=params(16),
    )(place, own, other, context)


def project_kernel(place, *refs):
    blocks, (rhs, give, keep, held) = refs[:NZ], refs[NZ:]
    _, _, core = where_am_i(place)
    lhs = jnp.concatenate([b[...] for b in blocks], axis=0)
    total = dot(lhs, rhs[...])
    spread = give.shape[0]
    rows = give.shape[1] // NZ
    total = total.reshape(NZ, spread, 2, rows, rhs.shape[1])
    for k in range(NZ):
        at = slice(k * rows, (k + 1) * rows)
        first, second = total[k, :, 0], total[k, :, 1]
        keep[:, at, :] = jnp.where(core == 0, first, second)
        held[:, at, :] = jnp.where(core == 0, second, first)
    give[...] = held[...].astype(BF16)


def project(place, blocks, rhs, spread):
    rows = blocks[0].shape[0] // (2 * spread)
    shape = (spread, NZ * rows, rhs.shape[1])
    return pl.pallas_call(
        project_kernel,
        out_shape=(jax.ShapeDtypeStruct(shape, BF16), jax.ShapeDtypeStruct(shape, F32)),
        in_specs=[SMEM] + [VMEM] * (NZ + 1),
        out_specs=(VMEM, VMEM),
        scratch_shapes=[pltpu.VMEM(shape, F32)],
        compiler_params=params(32),
    )(place, *blocks, rhs)


def join_kernel(keep, got, out):
    out[...] = (keep[...] + got[...].astype(F32)).astype(BF16)


def join(keep, got):
    return pl.pallas_call(
        join_kernel,
        out_shape=jax.ShapeDtypeStruct(keep.shape, BF16),
        in_specs=[VMEM] * 2,
        out_specs=VMEM,
        compiler_params=params(16),
    )(keep, got)


def settle_kernel(place, parts, ids, gates, out, held):
    z, _, _ = where_am_i(place)
    tokens = parts.shape[1]
    rows = tokens // NZ
    total = parts[0].astype(F32)
    for i in range(1, parts.shape[0]):
        total += parts[i].astype(F32)
    for k in range(NZ):
        at = pl.multiple_of(lax.rem(z + k, NZ) * rows, rows)
        held[pl.ds(at, rows), :] = total[k * rows : (k + 1) * rows]
    named = ids[...].astype(F32)
    high = gates[...].astype(BF16).astype(F32)
    low = gates[...] - high
    lane = lax.broadcasted_iota(jnp.int32, (rows, held.shape[1]), 1)
    note = jnp.zeros((rows, held.shape[1]), F32)
    for i, part in enumerate((named, high, low)):
        for k in range(TOPK):
            note = jnp.where(lane == i * TOPK + k, part[:, k : k + 1], note)
    held[tokens:, :] = note
    out[...] = held[...].astype(BF16)


def settle(place, parts, ids, gates):
    shape = (parts.shape[1] + ids.shape[0], parts.shape[2])
    return pl.pallas_call(
        settle_kernel,
        out_shape=jax.ShapeDtypeStruct(shape, BF16),
        in_specs=[SMEM, VMEM, VMEM, VMEM],
        out_specs=VMEM,
        scratch_shapes=[pltpu.VMEM(shape, F32)],
        compiler_params=params(16),
    )(place, parts, ids, gates)


def coords(index, axes):
    found = {}
    for axis in reversed(axes):
        size = SIZES[FINE.index(axis)]
        found[axis] = index % size
        index = index // size
    return found


def label_of(z, at):
    return (z * 2 + at["xl"]) * 4 + at["xh"] * 2 + at["y"] // 2


def routed(listed, label, spot):
    tokens, rows = listed.shape[0], ROWS
    match = jnp.zeros(label.shape, F32)
    gate = jnp.zeros(label.shape, F32)
    for k in range(TOPK):
        hit = listed[:, k : k + 1] == label.astype(F32)
        value = listed[:, TOPK + k : TOPK + k + 1] + listed[:, 2 * TOPK + k : 2 * TOPK + k + 1]
        match += jnp.where(hit, 1.0, 0.0)
        gate += jnp.where(hit, value, 0.0)
    before = lax.broadcasted_iota(jnp.int32, (tokens, tokens), 1)
    after = lax.broadcasted_iota(jnp.int32, (tokens, tokens), 0)
    earlier = (before // rows == after // rows) & (before < after)
    rank = dot(jnp.where(earlier, 1.0, 0.0).astype(BF16), match.astype(BF16))
    placed = (match > 0.5) & (rank.astype(jnp.int32) == spot)
    return placed, gate


def place_kernel(place, *refs):
    blocks, (gain, sent, own, high, low, stream, notes) = refs[:NZ], refs[NZ:]
    z, _, _ = where_am_i(place)
    pair, parity = lax.div(z, 2), lax.rem(z, 2)
    tokens, width = stream.shape
    rows, wide = ROWS, width // NZ
    lanes = sent.shape[0]
    for hop in range(NZ):
        there = lax.rem(z + hop, NZ)
        at = pl.multiple_of(there * wide, LANES)
        block = blocks[hop][...].astype(F32)
        stream[:, pl.ds(at, wide)] = block[:tokens]
        notes[pl.ds(pl.multiple_of(there * rows, rows), rows), :] = block[tokens:, :LANES]
    own[...] = stream[pl.ds(pl.multiple_of(z * rows, rows), rows), :]

    lane = lax.broadcasted_iota(jnp.int32, (tokens, lanes), 1)
    from_z = lax.broadcasted_iota(jnp.int32, (tokens, lanes), 0) // rows
    slot, device = lane % (NZ * CAP), lane // (NZ * CAP)
    label = label_of(z, coords(device, PLANE))
    spot = slot - (from_z % 2) * (NH * CAP) - (from_z // 2) * CAP
    placed, _ = routed(notes[...], label, spot)
    spots = jnp.transpose(jnp.where(placed, 1.0, 0.0)).astype(BF16)

    half = tokens // 2
    near = [lax.rem(pair + hop, NH) for hop in range(NH)]
    listed = jnp.concatenate(
        [notes[pl.ds(pl.multiple_of((2 * n + parity) * rows, rows), rows), :] for n in near],
        axis=0,
    )
    lane = lax.broadcasted_iota(jnp.int32, (half, lanes), 1)
    hop = lax.broadcasted_iota(jnp.int32, (half, lanes), 0) // rows
    slot, peer = lane % (NH * CAP), lane // (NH * CAP)
    at = coords(peer, PEERS)
    label = label_of(pair * 2 + at["zl"], at)
    placed, gate = routed(listed, label, slot - ((pair + hop) % NH) * CAP)
    weight = jnp.where(placed, gate, 0.0)
    top = weight.astype(BF16)
    high[...] = top
    low[...] = (weight - top.astype(F32)).astype(BF16)

    square = jnp.zeros((tokens, 1), F32)
    for i in range(NZ):
        part = stream[:, i * wide : (i + 1) * wide]
        square += jnp.sum(part * part, axis=-1, keepdims=True)
    scale = lax.rsqrt(square / width + 1e-06)
    for i in range(NZ):
        at = slice(i * wide, (i + 1) * wide)
        normed = (stream[:, at] * scale * gain[:, at]).astype(BF16)
        sent[:, at] = dot(spots, normed).astype(BF16)


def place_rows(place, blocks, gain, plane):
    tokens = NZ * ROWS
    width = NZ * blocks[0].shape[1]
    lanes = plane * NZ * CAP
    return pl.pallas_call(
        place_kernel,
        out_shape=(
            jax.ShapeDtypeStruct((lanes, width), BF16),
            jax.ShapeDtypeStruct((ROWS, width), F32),
            jax.ShapeDtypeStruct((tokens // 2, lanes), BF16),
            jax.ShapeDtypeStruct((tokens // 2, lanes), BF16),
        ),
        in_specs=[SMEM] + [VMEM] * (NZ + 1),
        out_specs=(VMEM,) * 4,
        scratch_shapes=[
            pltpu.VMEM((tokens, width), F32),
            pltpu.VMEM((tokens, LANES), F32),
        ],
        compiler_params=params(32),
    )(place, *blocks, gain.reshape(1, width))


def expert_kernel(first, rows, w_gate, w_up, w_down, out):
    count, width = out.shape
    deep = width // 4
    piece = rows[first : first + count, :]
    gate_act = dot(piece, w_gate[0])
    up_act = dot(piece, w_up[0])
    hidden = (jax.nn.silu(gate_act) * up_act).astype(BF16)
    for i in range(4):
        at = slice(i * deep, (i + 1) * deep)
        out[:, at] = dot(hidden, w_down[0, :, at]).astype(BF16)


def expert_rows(rows, first, count, w_gate, w_up, w_down):
    return pl.pallas_call(
        functools.partial(expert_kernel, first),
        out_shape=jax.ShapeDtypeStruct((count, rows.shape[1]), BF16),
        in_specs=[VMEM] * 4,
        out_specs=VMEM,
        compiler_params=params(32),
        cost_estimate=pl.CostEstimate(
            flops=6 * count * w_down.shape[1] * w_down.shape[2],
            bytes_accessed=6 * w_down.size + 4 * count * rows.shape[1],
            transcendentals=count * w_down.shape[1],
        ),
    )(rows, w_gate, w_up, w_down)


def add_kernel(first, mine, part, *refs):
    out = refs[-1]
    count = part.shape[0]
    if len(refs) > 1:
        out[:first, :] = refs[0][...]
    total = mine[first : first + count, :].astype(F32) + part[...].astype(F32)
    out[first:, :] = total.astype(BF16)


def add_rows(mine, part, *before):
    first = before[0].shape[0] if before else 0
    return pl.pallas_call(
        functools.partial(add_kernel, first),
        out_shape=jax.ShapeDtypeStruct((first + part.shape[0], mine.shape[1]), BF16),
        in_specs=[VMEM] * (2 + len(before)),
        out_specs=VMEM,
        compiler_params=params(32),
    )(mine, part, *before)


def combine_kernel(high, low, back, own, base, *outs):
    rows, width = own.shape
    wide = width // 4
    for i in range(4):
        at = slice(i * wide, (i + 1) * wide)
        piece = back[:, at]
        mix = dot(high[...], piece) + dot(low[...], piece)
        base[:, at] = own[:, at] + mix[:rows]
        for hop in range(1, NH):
            outs[hop - 1][:, at] = mix[hop * rows : (hop + 1) * rows].astype(BF16)


def combine(high, low, back, own):
    rows, width = own.shape
    return pl.pallas_call(
        combine_kernel,
        out_shape=(jax.ShapeDtypeStruct((rows, width), F32),)
        + (jax.ShapeDtypeStruct((rows, width), BF16),) * (NH - 1),
        in_specs=[VMEM] * 4,
        out_specs=(VMEM,) * NH,
        compiler_params=params(32),
    )(high, low, back, own)


def on_device(context, proj_weight, norm_gain, expert_ids, gate_values, w_gate, w_up, w_down):
    zi, xli, ci = (lax.axis_index(a).astype(jnp.int32) for a in (RING, "xl", "c"))
    place = (4 * zi + 2 * xli + ci).reshape(1)
    n_spread = lax.axis_size(SPREAD)
    n_plane, n_peers = lax.axis_size(PLANE), lax.axis_size(PEERS)

    rhs, held = stage(place, proj_weight, swap(proj_weight, "xl"), context)
    give, keep = project(place, [held] + gather_z(context)[1:], rhs, n_spread)
    partial = join(keep, swap(give, "c"))
    partial = lax.all_to_all(partial, SPREAD, 0, 0, tiled=True)

    part = settle(place, partial, expert_ids, gate_values)
    sent, own, high, low = place_rows(place, gather_z(part), norm_gain, n_plane)
    width = sent.shape[1]
    mine = lax.all_to_all(sent.reshape(n_plane, -1, width), PLANE, 0, 0, tiled=True)
    mine = mine.reshape(-1, width)

    weights = (w_gate, w_up, w_down)
    theirs = swap(mine, "c")
    count = mine.shape[0]
    mine_out = expert_rows(mine, 0, count, *weights)
    theirs, mine_out = lax.optimization_barrier((theirs, mine_out))
    half = count // 2
    top, bottom = (swap(expert_rows(theirs, at, half, *weights), "c") for at in (0, half))
    summed = add_rows(mine_out, bottom, add_rows(mine_out, top)).reshape(n_peers, -1, width)
    back = lax.all_to_all(summed, PEERS, 0, 0, tiled=True).reshape(-1, width)

    total, *blocks = combine(high, low, back, own)
    for hop in (2, 1, 3):
        total += fetch_pair(blocks[hop - 1], -hop).astype(F32)
    return total.astype(BF16)


def solution(mesh):
    fine = Mesh(mesh.devices.reshape(SIZES), FINE)
    both = EXPERT + TENSOR
    return jax.shard_map(
        on_device,
        mesh=fine,
        in_specs=(
            P(EXPERT, TENSOR),
            P(TENSOR, EXPERT),
            P(),
            P(both, None),
            P(both, None),
            P(both, None, None),
            P(both, None, None),
            P(both, None, None),
        ),
        out_specs=P(both, None),
        check_vma=False,
    )
```

```python
import functools

import jax
import jax.numpy as jnp
from jax import lax
from jax.experimental import pallas as pl
from jax.experimental.pallas import tpu as pltpu
from jax.sharding import Mesh
from jax.sharding import PartitionSpec as P

TOPK = 8
CAP = 2
ROWS = 8
LANES = 128
F32, BF16 = jnp.float32, jnp.bfloat16

FINE = ("zh", "zl", "xl", "xh", "y", "c")
SIZES = (4, 2, 2, 2, 4, 2)
EXPERT = ("zh", "zl", "xl")
TENSOR = ("xh", "y", "c")
SPREAD = ("xh", "y")
PLANE = ("y", "xl", "xh")
PEERS = ("y", "xl", "xh", "zl")
RING = ("zh", "zl")
NZ, NH = 8, 4
MIB = 1 << 20

VMEM = pl.BlockSpec(memory_space=pltpu.VMEM)
SMEM = pl.BlockSpec(memory_space=pltpu.SMEM)


def swap(x, axis):
    return lax.ppermute(x, axis, [(0, 1), (1, 0)])


def fetch(x, hop, axis=RING, size=NZ):
    return lax.ppermute(x, axis, [((i + hop) % size, i) for i in range(size)])


def fetch_pair(x, hop):
    return fetch(x, hop, "zh", NH)


def gather_z(x):
    up2, dn2 = fetch(x, 2), fetch(x, -2)
    up1, dn1 = fetch(x, 1), fetch(x, -1)
    up3, dn3 = fetch(up2, 1), fetch(dn2, -1)
    far = fetch(up2, 2)
    return [x, up1, up2, up3, far, dn3, dn2, dn1]


def params(mib):
    return pltpu.CompilerParams(vmem_limit_bytes=mib * MIB)


def dot(a, b):
    return jnp.dot(a, b, preferred_element_type=F32)


def where_am_i(place):
    return lax.div(place[0], 4), lax.rem(lax.div(place[0], 2), 2), lax.rem(place[0], 2)


def stage_kernel(place, own, other, context, rhs, held):
    _, xl, _ = where_am_i(place)
    cols = own.shape[1]
    rhs[:, pl.ds(pl.multiple_of(xl * cols, LANES), cols)] = own[...]
    rhs[:, pl.ds(pl.multiple_of((1 - xl) * cols, LANES), cols)] = other[...]
    held[...] = context[...]


def stage(place, own, other, context):
    return pl.pallas_call(
        stage_kernel,
        out_shape=(
            jax.ShapeDtypeStruct((own.shape[0], 2 * own.shape[1]), BF16),
            jax.ShapeDtypeStruct(context.shape, BF16),
        ),
        in_specs=[SMEM] + [VMEM] * 3,
        out_specs=(VMEM, VMEM),
        compiler_params=params(16),
    )(place, own, other, context)


def project_kernel(place, *refs):
    blocks, (rhs, give, keep, held) = refs[:NZ], refs[NZ:]
    _, _, core = where_am_i(place)
    lhs = jnp.concatenate([b[...] for b in blocks], axis=0)
    total = dot(lhs, rhs[...])
    spread = give.shape[0]
    rows = give.shape[1] // NZ
    total = total.reshape(NZ, spread, 2, rows, rhs.shape[1])
    for k in range(NZ):
        at = slice(k * rows, (k + 1) * rows)
        first, second = total[k, :, 0], total[k, :, 1]
        keep[:, at, :] = jnp.where(core == 0, first, second)
        held[:, at, :] = jnp.where(core == 0, second, first)
    give[...] = held[...].astype(BF16)


def project(place, blocks, rhs, spread):
    rows = blocks[0].shape[0] // (2 * spread)
    shape = (spread, NZ * rows, rhs.shape[1])
    return pl.pallas_call(
        project_kernel,
        out_shape=(jax.ShapeDtypeStruct(shape, BF16), jax.ShapeDtypeStruct(shape, F32)),
        in_specs=[SMEM] + [VMEM] * (NZ + 1),
        out_specs=(VMEM, VMEM),
        scratch_shapes=[pltpu.VMEM(shape, F32)],
        compiler_params=params(32),
    )(place, *blocks, rhs)


def join_kernel(keep, got, out):
    out[...] = (keep[...] + got[...].astype(F32)).astype(BF16)


def join(keep, got):
    return pl.pallas_call(
        join_kernel,
        out_shape=jax.ShapeDtypeStruct(keep.shape, BF16),
        in_specs=[VMEM] * 2,
        out_specs=VMEM,
        compiler_params=params(16),
    )(keep, got)


def settle_kernel(place, parts, ids, gates, out, held):
    z, _, _ = where_am_i(place)
    tokens = parts.shape[1]
    rows = tokens // NZ
    total = parts[0].astype(F32)
    for i in range(1, parts.shape[0]):
        total += parts[i].astype(F32)
    for k in range(NZ):
        at = pl.multiple_of(lax.rem(z + k, NZ) * rows, rows)
        held[pl.ds(at, rows), :] = total[k * rows : (k + 1) * rows]
    named = ids[...].astype(F32)
    high = gates[...].astype(BF16).astype(F32)
    low = gates[...] - high
    lane = lax.broadcasted_iota(jnp.int32, (rows, held.shape[1]), 1)
    note = jnp.zeros((rows, held.shape[1]), F32)
    for i, part in enumerate((named, high, low)):
        for k in range(TOPK):
            note = jnp.where(lane == i * TOPK + k, part[:, k : k + 1], note)
    held[tokens:, :] = note
    out[...] = held[...].astype(BF16)


def settle(place, parts, ids, gates):
    shape = (parts.shape[1] + ids.shape[0], parts.shape[2])
    return pl.pallas_call(
        settle_kernel,
        out_shape=jax.ShapeDtypeStruct(shape, BF16),
        in_specs=[SMEM, VMEM, VMEM, VMEM],
        out_specs=VMEM,
        scratch_shapes=[pltpu.VMEM(shape, F32)],
        compiler_params=params(16),
    )(place, parts, ids, gates)


def coords(index, axes):
    found = {}
    for axis in reversed(axes):
        size = SIZES[FINE.index(axis)]
        found[axis] = index % size
        index = index // size
    return found


def label_of(z, at):
    return (z * 2 + at["xl"]) * 4 + at["xh"] * 2 + at["y"] // 2


def routed(listed, label, spot):
    tokens, rows = listed.shape[0], ROWS
    match = jnp.zeros(label.shape, F32)
    gate = jnp.zeros(label.shape, F32)
    for k in range(TOPK):
        hit = listed[:, k : k + 1] == label.astype(F32)
        value = listed[:, TOPK + k : TOPK + k + 1] + listed[:, 2 * TOPK + k : 2 * TOPK + k + 1]
        match += jnp.where(hit, 1.0, 0.0)
        gate += jnp.where(hit, value, 0.0)
    before = lax.broadcasted_iota(jnp.int32, (tokens, tokens), 1)
    after = lax.broadcasted_iota(jnp.int32, (tokens, tokens), 0)
    earlier = (before // rows == after // rows) & (before < after)
    rank = dot(jnp.where(earlier, 1.0, 0.0).astype(BF16), match.astype(BF16))
    placed = (match > 0.5) & (rank.astype(jnp.int32) == spot)
    return placed, gate


def place_kernel(place, *refs):
    blocks, (gain, sent, own, high, low, stream, notes) = refs[:NZ], refs[NZ:]
    z, _, _ = where_am_i(place)
    pair, parity = lax.div(z, 2), lax.rem(z, 2)
    tokens, width = stream.shape
    rows, wide = ROWS, width // NZ
    lanes = sent.shape[0]
    for hop in range(NZ):
        there = lax.rem(z + hop, NZ)
        at = pl.multiple_of(there * wide, LANES)
        block = blocks[hop][...].astype(F32)
        stream[:, pl.ds(at, wide)] = block[:tokens]
        notes[pl.ds(pl.multiple_of(there * rows, rows), rows), :] = block[tokens:, :LANES]
    own[...] = stream[pl.ds(pl.multiple_of(z * rows, rows), rows), :]

    lane = lax.broadcasted_iota(jnp.int32, (tokens, lanes), 1)
    from_z = lax.broadcasted_iota(jnp.int32, (tokens, lanes), 0) // rows
    slot, device = lane % (NZ * CAP), lane // (NZ * CAP)
    label = label_of(z, coords(device, PLANE))
    spot = slot - (from_z % 2) * (NH * CAP) - (from_z // 2) * CAP
    placed, _ = routed(notes[...], label, spot)
    spots = jnp.transpose(jnp.where(placed, 1.0, 0.0)).astype(BF16)

    half = tokens // 2
    near = [lax.rem(pair + hop, NH) for hop in range(NH)]
    listed = jnp.concatenate(
        [notes[pl.ds(pl.multiple_of((2 * n + parity) * rows, rows), rows), :] for n in near],
        axis=0,
    )
    lane = lax.broadcasted_iota(jnp.int32, (half, lanes), 1)
    hop = lax.broadcasted_iota(jnp.int32, (half, lanes), 0) // rows
    slot, peer = lane % (NH * CAP), lane // (NH * CAP)
    at = coords(peer, PEERS)
    label = label_of(pair * 2 + at["zl"], at)
    placed, gate = routed(listed, label, slot - ((pair + hop) % NH) * CAP)
    weight = jnp.where(placed, gate, 0.0)
    top = weight.astype(BF16)
    high[...] = top
    low[...] = (weight - top.astype(F32)).astype(BF16)

    square = jnp.zeros((tokens, 1), F32)
    for i in range(NZ):
        part = stream[:, i * wide : (i + 1) * wide]
        square += jnp.sum(part * part, axis=-1, keepdims=True)
    scale = lax.rsqrt(square / width + 1e-06)
    for i in range(NZ):
        at = slice(i * wide, (i + 1) * wide)
        normed = (stream[:, at] * scale * gain[:, at]).astype(BF16)
        sent[:, at] = dot(spots, normed).astype(BF16)


def place_rows(place, blocks, gain, plane):
    tokens = NZ * ROWS
    width = NZ * blocks[0].shape[1]
    lanes = plane * NZ * CAP
    return pl.pallas_call(
        place_kernel,
        out_shape=(
            jax.ShapeDtypeStruct((lanes, width), BF16),
            jax.ShapeDtypeStruct((ROWS, width), F32),
            jax.ShapeDtypeStruct((tokens // 2, lanes), BF16),
            jax.ShapeDtypeStruct((tokens // 2, lanes), BF16),
        ),
        in_specs=[SMEM] + [VMEM] * (NZ + 1),
        out_specs=(VMEM,) * 4,
        scratch_shapes=[
            pltpu.VMEM((tokens, width), F32),
            pltpu.VMEM((tokens, LANES), F32),
        ],
        compiler_params=params(32),
    )(place, *blocks, gain.reshape(1, width))


def expert_kernel(first, rows, w_gate, w_up, w_down, out):
    count, width = out.shape
    deep = width // 4
    piece = rows[first : first + count, :]
    gate_act = dot(piece, w_gate[0])
    up_act = dot(piece, w_up[0])
    hidden = (jax.nn.silu(gate_act) * up_act).astype(BF16)
    for i in range(4):
        at = slice(i * deep, (i + 1) * deep)
        out[:, at] = dot(hidden, w_down[0, :, at]).astype(BF16)


def expert_rows(rows, first, count, w_gate, w_up, w_down):
    return pl.pallas_call(
        functools.partial(expert_kernel, first),
        out_shape=jax.ShapeDtypeStruct((count, rows.shape[1]), BF16),
        in_specs=[VMEM] * 4,
        out_specs=VMEM,
        compiler_params=params(32),
        cost_estimate=pl.CostEstimate(
            flops=6 * count * w_down.shape[1] * w_down.shape[2],
            bytes_accessed=6 * w_down.size + 4 * count * rows.shape[1],
            transcendentals=count * w_down.shape[1],
        ),
    )(rows, w_gate, w_up, w_down)


def add_kernel(first, mine, part, *refs):
    out = refs[-1]
    count = part.shape[0]
    if len(refs) > 1:
        out[:first, :] = refs[0][...]
    total = mine[first : first + count, :].astype(F32) + part[...].astype(F32)
    out[first:, :] = total.astype(BF16)


def add_rows(mine, part, *before):
    first = before[0].shape[0] if before else 0
    return pl.pallas_call(
        functools.partial(add_kernel, first),
        out_shape=jax.ShapeDtypeStruct((first + part.shape[0], mine.shape[1]), BF16),
        in_specs=[VMEM] * (2 + len(before)),
        out_specs=VMEM,
        compiler_params=params(32),
    )(mine, part, *before)


def combine_kernel(high, low, back, own, base, *outs):
    rows, width = own.shape
    wide = width // 4
    for i in range(4):
        at = slice(i * wide, (i + 1) * wide)
        piece = back[:, at]
        mix = dot(high[...], piece) + dot(low[...], piece)
        base[:, at] = own[:, at] + mix[:rows]
        for hop in range(1, NH):
            outs[hop - 1][:, at] = mix[hop * rows : (hop + 1) * rows].astype(BF16)


def combine(high, low, back, own):
    rows, width = own.shape
    return pl.pallas_call(
        combine_kernel,
        out_shape=(jax.ShapeDtypeStruct((rows, width), F32),)
        + (jax.ShapeDtypeStruct((rows, width), BF16),) * (NH - 1),
        in_specs=[VMEM] * 4,
        out_specs=(VMEM,) * NH,
        compiler_params=params(32),
    )(high, low, back, own)


def finish_kernel(base, *refs):
    out = refs[-1]
    total = base[...]
    for part in refs[:-1]:
        total += part[...].astype(F32)
    out[...] = total.astype(BF16)


def finish(base, parts):
    return pl.pallas_call(
        finish_kernel,
        out_shape=jax.ShapeDtypeStruct(base.shape, BF16),
        in_specs=[VMEM] * (1 + len(parts)),
        out_specs=VMEM,
        compiler_params=params(16),
    )(base, *parts)


def on_device(context, proj_weight, norm_gain, expert_ids, gate_values, w_gate, w_up, w_down):
    zi, xli, ci = (lax.axis_index(a).astype(jnp.int32) for a in (RING, "xl", "c"))
    place = (4 * zi + 2 * xli + ci).reshape(1)
    n_spread = lax.axis_size(SPREAD)
    n_plane, n_peers = lax.axis_size(PLANE), lax.axis_size(PEERS)

    rhs, held = stage(place, proj_weight, swap(proj_weight, "xl"), context)
    give, keep = project(place, [held] + gather_z(context)[1:], rhs, n_spread)
    partial = join(keep, swap(give, "c"))
    partial = lax.all_to_all(partial, SPREAD, 0, 0, tiled=True)

    part = settle(place, partial, expert_ids, gate_values)
    sent, own, high, low = place_rows(place, gather_z(part), norm_gain, n_plane)
    width = sent.shape[1]
    mine = lax.all_to_all(sent.reshape(n_plane, -1, width), PLANE, 0, 0, tiled=True)
    mine = mine.reshape(-1, width)

    weights = (w_gate, w_up, w_down)
    theirs = swap(mine, "c")
    count = mine.shape[0]
    mine_out = expert_rows(mine, 0, count, *weights)
    theirs, mine_out = lax.optimization_barrier((theirs, mine_out))
    half = count // 2
    top, bottom = (swap(expert_rows(theirs, at, half, *weights), "c") for at in (0, half))
    summed = add_rows(mine_out, bottom, add_rows(mine_out, top)).reshape(n_peers, -1, width)
    back = lax.all_to_all(summed, PEERS, 0, 0, tiled=True).reshape(-1, width)

    base, *blocks = combine(high, low, back, own)
    return finish(base, [fetch_pair(blocks[hop - 1], -hop) for hop in (2, 1, 3)])


def solution(mesh):
    fine = Mesh(mesh.devices.reshape(SIZES), FINE)
    both = EXPERT + TENSOR
    return jax.shard_map(
        on_device,
        mesh=fine,
        in_specs=(
            P(EXPERT, TENSOR),
            P(TENSOR, EXPERT),
            P(),
            P(both, None),
            P(both, None),
            P(both, None, None),
            P(both, None, None),
            P(both, None, None),
        ),
        out_specs=P(both, None),
        check_vma=False,
    )
```
